128 devices in a mesh: px: 8 (over z, x_lo), py: 16 (over x_hi, y, core).
Axes of the slice: x: 4 (x_hi: 2, x_lo: 2; x = x_hi * 2 + x_lo), y: 4, z: 4, core: 2. Of those that a mesh axis runs over, the one named last changes fastest.
Arguments:
- loads: float32 [3, 128, 1024, 128], P(None, 'px', 'py'), may hold values from -6 to 6
- targets: float32 [3, 128, 1024, 128], P(None, 'px', 'py'), may hold values from -6 to 6
- anchor: float32 [128, 1024], P('px', 'py'), may hold values from 0.05 to 0.5
- q_down: float32 [128, 1024], P('px', 'py'), may hold values from 0.5 to 2
- q_right: float32 [128, 1024], P('px', 'py'), may hold values from 0.5 to 2
- send_rows: int32 [8, 1024], P('px', 'py'), may hold values from 0 to 1023, as said below
- cable_a: int32 [8, 2048], P('px', 'py'), may hold values from 0 to 63, as said below
- cable_b: int32 [8, 2048], P('px', 'py'), may hold values from 0 to 63, as said below
- cable_count: int32 [8, 16], P('px', 'py'), may hold values from 1 to 128, 1024 in all within a row
- cable_q: float32 [8, 2048], P('px', 'py'), may hold values from 0.5 to 2
Outputs:
- shape_field: float32 [3, 128, 1024, 128], P(None, 'px', 'py')
- adjoint_field: float32 [3, 128, 1024, 128], P(None, 'px', 'py')
- grad_down: float32 [128, 1024], P('px', 'py')
- grad_right: float32 [128, 1024], P('px', 'py')
- grad_long: float32 [8, 2048], P('px', 'py')
The draws below stay inside these ranges and needn't reach their ends.
Inputs may be any that keep to these rules, and one draw needn't show every extreme that they name: `send_rows`: within each block of 4 entries (one tile lending to one owner) the nodes differ. `cable_a`: codes of one cable's two ends differ. `cable_b`: codes of one cable's two ends differ. `cable_count`: each plan-x row's counts sum to 1024; some owner has all 128 slots live.
All inputs are finite; a program needn't handle non-finite values. No bound on the sum of `cable_count` on one device may be relied on, other than what follows from the above.
Results may differ from the reference program's by a relative error of at most 0.00011.
Values sent between devices are 32-bit elements; how exact they have to be, the bound alone decides.
A program may use at most 128 MiB of HBM per device.

```python
import math
import jax
import jax.numpy as jnp
import numpy as np

TX = 16
TY = 64
V = 128
SLOT = 4
CAB_DEV = 128
STEPS = 7
NX = 128
NY = 1024
RECV = 64
CABLES = 2048
N_PX = 8
N_PY = 16


def draw_send_rows(key, part):
    node_count = TX * TY
    stride = node_count // SLOT
    key_base, key_offset = jax.random.split(jax.random.fold_in(key, 11))
    base = jax.random.randint(key_base, (N_PX, N_PY * N_PY, 1), 0, node_count)
    offset = jax.random.randint(key_offset, (N_PX, N_PY * N_PY, SLOT), 0, stride)
    slots = jnp.arange(SLOT, dtype=jnp.int32)[None, None, :]
    nodes = (base + slots * stride + offset) % node_count
    return nodes.reshape(N_PX, N_PY * N_PY * SLOT).astype(jnp.int32)


def cable_pair(key):
    key_first, key_step = jax.random.split(jax.random.fold_in(key, 23))
    first = jax.random.randint(key_first, (N_PX, N_PY * CAB_DEV), 0, RECV)
    step = jax.random.randint(key_step, (N_PX, N_PY * CAB_DEV), 1, RECV)
    second = (first + step) % RECV
    return (first.astype(jnp.int32), second.astype(jnp.int32))


def draw_cable_a(key, part):
    return cable_pair(key)[0]


def draw_cable_b(key, part):
    return cable_pair(key)[1]


def steps_of(key, extent, cuts, low, top_value):
    loudness, own = 1.0, jax.random.fold_in(key, 6)
    for dim, blocks in cuts:
        draws = jnp.exp(jax.random.uniform(jax.random.fold_in(own, dim), (blocks,), jnp.float32, low / len(cuts), top_value / len(cuts)))
        loudness = loudness * jnp.repeat(draws, extent[dim] // blocks).reshape([-1 if axis == dim else 1 for axis in range(len(extent))])
    return loudness


def profile(amount, total, limit, skew):
    weights = [(1 << 20) // math.isqrt(grade ** skew) + 1 for grade in range(2, amount + 1)]
    surplus, given = total - limit - (amount - 1), [1] * (amount - 1)
    while surplus > 0:
        movable = [i for i in range(amount - 1) if given[i] < limit]
        whole, left = sum([weights[i] for i in movable]), surplus
        for i in movable:
            addition = min(limit - given[i], max(1, left * weights[i] // whole), surplus)
            given[i] = given[i] + addition
            surplus = surplus - addition
    return np.array([limit] + given)


def ragged_sizes(own_key, number_of, total, limit, slope):
    if number_of == 2:
        one = jax.random.randint(own_key, (), max(1, total - limit), min(limit, total - 1) + 1)
        return jnp.stack([one, total - one])
    tallies = jnp.asarray(profile(number_of, total, limit, slope), jnp.int32)
    couples = (number_of - 1) // 2
    source_of, sink = tallies[1:1 + 2 * couples:2], tallies[2:2 + 2 * couples:2]
    margin = jnp.minimum(source_of - 1, limit - sink)
    passed = jax.random.randint(jax.random.fold_in(own_key, 1), (couples,), 0, 1 << 20) % (margin + 1)
    tallies = tallies.at[1:1 + 2 * couples:2].set(source_of - passed).at[2:2 + 2 * couples:2].set(sink + passed)
    return tallies[jax.random.permutation(jax.random.fold_in(own_key, 2), number_of)]


def centred(own_key, shape, deviation, bound, cuts=(), held_as=jnp.bfloat16):
    entries = jax.random.normal(own_key, shape, jnp.float32) * deviation
    if len(cuts) > 0:
        entries = steps_of(own_key, shape, cuts, -0.22, 0.18) * entries
    return jnp.clip(entries, min=-bound, max=bound).astype(held_as)


def setup_inputs(seed: int = 0) -> dict:
    key_of = jax.random.split(jax.random.key(seed), 11)
    return {
        "loads": centred(key_of[0], (3, NX, NY, V), 1.0, 6.0, ((1, 8), (2, 16)), jnp.float32),
        "targets": centred(key_of[1], (3, NX, NY, V), 1.0, 6.0, ((1, 8), (2, 16)), jnp.float32),
        "anchor": jnp.clip(jnp.exp(math.log(0.5) - 2.3025851 * jax.random.uniform(key_of[2], (NX, NY), jnp.float32) ** steps_of(key_of[2], (NX, NY), ((0, 8), (1, 16)), -0.2, 0.2)), 0.05, 0.5),
        "q_down": jnp.clip(jnp.exp(math.log(2.0) - 1.3862944 * jax.random.uniform(key_of[3], (NX, NY), jnp.float32) ** steps_of(key_of[3], (NX, NY), ((0, 8), (1, 16)), -0.2, 0.2)), 0.5, 2.0),
        "q_right": jnp.clip(jnp.exp(math.log(2.0) - 1.3862944 * jax.random.uniform(key_of[4], (NX, NY), jnp.float32) ** steps_of(key_of[4], (NX, NY), ((0, 8), (1, 16)), -0.2, 0.2)), 0.5, 2.0),
        "send_rows": draw_send_rows(jax.random.fold_in(key_of[10], 71), 0),
        "cable_a": draw_cable_a(jax.random.fold_in(key_of[10], 71), 0),
        "cable_b": draw_cable_b(jax.random.fold_in(key_of[10], 71), 0),
        "cable_count": jax.vmap(lambda own: ragged_sizes(own, N_PY, N_PY * CAB_DEV // 2, CAB_DEV, 2))(jax.random.split(key_of[8], N_PX)).reshape((N_PX, N_PY)).astype(jnp.int32),
        "cable_q": jnp.clip(jnp.exp(math.log(2.0) - 1.3862944 * jax.random.uniform(key_of[9], (N_PX, CABLES), jnp.float32) ** steps_of(key_of[9], (N_PX, CABLES), ((0, 8), (1, 16)), -0.2, 0.2)), 0.5, 2.0),
    }


cheb_low = 0.05
cheb_high = 2.0


def chebyshev(rhs, operate, inv_diag):
    theta = (cheb_high + cheb_low) / 2.0
    delta = (cheb_high - cheb_low) / 2.0
    sigma = theta / delta
    rho = 1.0 / sigma
    direction = inv_diag * rhs / theta
    solution = jnp.zeros_like(rhs)
    resid = rhs
    for step in range(STEPS):
        solution = solution + direction
        if step + 1 < STEPS:
            resid = resid - operate(direction)
            rho_new = 1.0 / (2.0 * sigma - rho)
            direction = (rho_new * rho) * direction + (2.0 * rho_new / delta) * (inv_diag * resid)
            rho = rho_new
    return solution


def reference(loads, targets, anchor, q_down, q_right, send_rows, cable_a, cable_b, cable_count, cable_q):
    grow = jnp.arange(NX, dtype=jnp.int32)[:, None]
    gcol = jnp.arange(NY, dtype=jnp.int32)[None, :]
    mask_down = grow < NX - 1
    mask_right = gcol < NY - 1
    w_down = jnp.where(mask_down, q_down, 0.0)
    w_right = jnp.where(mask_right, q_right, 0.0)
    w_up = jnp.pad(w_down, ((1, 0), (0, 0)))[:-1]
    w_left = jnp.pad(w_right, ((0, 0), (1, 0)))[:, :-1]
    grid_diag = anchor + w_down + w_up + w_right + w_left

    slot_ids = jnp.arange(CAB_DEV, dtype=jnp.int32)[None, None, :]
    live = slot_ids < cable_count[:, :, None]
    q_long = jnp.where(live, cable_q.reshape(N_PX, N_PY, CAB_DEV), 0.0)
    q_flat = q_long.reshape(-1)
    table = send_rows.reshape(N_PX, N_PY, N_PY, SLOT)
    row_ids = jnp.arange(N_PX, dtype=jnp.int32)[:, None, None]
    owner_ids = jnp.arange(N_PY, dtype=jnp.int32)[None, :, None]

    def flat_id(ends):
        ends3 = ends.reshape(N_PX, N_PY, CAB_DEV)
        source = ends3 // SLOT
        within = ends3 % SLOT
        local = table[row_ids, source, owner_ids, within]
        node_x = row_ids * TX + local // TY
        node_y = source * TY + local % TY
        return (node_x * NY + node_y).reshape(-1).astype(jnp.int32)

    index_a = flat_id(cable_a)
    index_b = flat_id(cable_b)
    long_diag = jnp.zeros((NX * NY,), jnp.float32).at[index_a].add(q_flat).at[index_b].add(q_flat)
    inv_diag = 1.0 / (grid_diag + long_diag.reshape(NX, NY))
    inv_full = inv_diag[None, :, :, None]

    def weigh(weight):
        return weight[None, :, :, None]

    def operate(field):
        padded = jnp.pad(field, ((0, 0), (1, 1), (1, 1), (0, 0)))
        near = weigh(w_down) * padded[:, 2:, 1:-1] + weigh(w_up) * padded[:, :-2, 1:-1]
        near = near + weigh(w_right) * padded[:, 1:-1, 2:] + weigh(w_left) * padded[:, 1:-1, :-2]
        flat = field.reshape(3, NX * NY, V)
        force = q_flat[None, :, None] * (flat[:, index_a] - flat[:, index_b])
        long_term = jnp.zeros((3, NX * NY, V), jnp.float32).at[:, index_a].add(force).at[:, index_b].add(-force)
        return weigh(grid_diag) * field - near + long_term.reshape(3, NX, NY, V)

    shape_field = chebyshev(loads, operate, inv_full)
    adjoint_field = chebyshev(shape_field - targets, operate, inv_full)

    pad_x = jnp.pad(shape_field, ((0, 0), (0, 1), (0, 1), (0, 0)))
    pad_l = jnp.pad(adjoint_field, ((0, 0), (0, 1), (0, 1), (0, 0)))
    dx_down = shape_field - pad_x[:, 1:, :-1]
    dl_down = adjoint_field - pad_l[:, 1:, :-1]
    dx_right = shape_field - pad_x[:, :-1, 1:]
    dl_right = adjoint_field - pad_l[:, :-1, 1:]
    grad_down = jnp.where(mask_down, -jnp.sum(dx_down * dl_down, axis=(0, 3)) / V, 0.0)
    grad_right = jnp.where(mask_right, -jnp.sum(dx_right * dl_right, axis=(0, 3)) / V, 0.0)

    flat_x = shape_field.reshape(3, NX * NY, V)
    flat_l = adjoint_field.reshape(3, NX * NY, V)
    dx_long = flat_x[:, index_a] - flat_x[:, index_b]
    dl_long = flat_l[:, index_a] - flat_l[:, index_b]
    grad_flat = -jnp.sum(dx_long * dl_long, axis=(0, 2)) / V
    grad_long = jnp.where(live.reshape(-1), grad_flat, 0.0).reshape(N_PX, CABLES)
    return shape_field, adjoint_field, grad_down, grad_right, grad_long
```

```python
import functools

import jax
import jax.numpy as jnp
from jax import lax
from jax.experimental import pallas as pl
from jax.experimental.pallas import tpu as pltpu
from jax.sharding import PartitionSpec as P

MESH = pl.DeviceIdType.MESH
F32 = jnp.float32
BF16 = jnp.bfloat16
HIGHEST = lax.Precision.HIGHEST

STEPS = 7
ROUNDS = STEPS - 1
TX, TY, V = 16, 64, 128
NODES = TX * TY
SLOTS = 64
LOW, HIGH = 0.05, 2.0
THETA = (HIGH + LOW) / 2.0
DELTA = (HIGH - LOW) / 2.0


def coefficients():
    sigma = THETA / DELTA
    rho = 1.0 / sigma
    pairs = []
    for _ in range(ROUNDS):
        rho_new = 1.0 / (2.0 * sigma - rho)
        pairs.append((rho_new * rho, 2.0 * rho_new / DELTA))
        rho = rho_new
    return pairs


COEF = coefficients()


def coef_of(round_):
    a, b = (jnp.float32(value) for value in COEF[-1])
    for k in range(ROUNDS - 1):
        a = jnp.where(round_ == k, jnp.float32(COEF[k][0]), a)
        b = jnp.where(round_ == k, jnp.float32(COEF[k][1]), b)
    return a, b


def split2(x):
    high = x.astype(BF16)
    return high, (x - high.astype(F32)).astype(BF16)


def split3(x):
    high = x.astype(BF16)
    rest = x - high.astype(F32)
    mid = rest.astype(BF16)
    return high, mid, (rest - mid.astype(F32)).astype(BF16)


def dot(a, b):
    return jnp.dot(a, b, preferred_element_type=F32)


def dot_t(a, b, precision=None):
    return lax.dot_general(
        a, b, (((1,), (1,)), ((), ())), precision=precision, preferred_element_type=F32
    )


def iota(shape, dim):
    return lax.broadcasted_iota(jnp.int32, shape, dim)


(
    S_P1, R_P1, S_P2, R_P2, S_UP, R_UP, S_DN, R_DN, S_LF, R_LF, S_RT, R_RT,
    S_CAB, R_CAB, S_DQ, R_DQ, S_QD, R_QD, S_QR, R_QR, S_SH, R_SH,
    S_GD, R_GD, S_GR, R_GR, S_HD, R_HD, S_HR, R_HR, L_B, L_T, L_S, L_A,
) = range(0, 68, 2)
N_SEM = 68


def kernel(
    n_px, n_py,
    loads, targets, anchor, q_down, q_right, rows_s, rows_v, cab_a, cab_b, count, cab_q,
    shape_out, adjoint_out, down_out, right_out, long_out,
    R, D, X, S, T, SF, GD, WD, WR, WL, INV, ONE, F3, C3, LH, LL, LM,
    rg_l, d_l, x_l, t_l, inv_l, Y, XS, recv1, recvS, Fs, frecv,
    up, dn, lf, rt, cl, cr, cab_s, cab_r, dq_s, dq_r, qd_s, qd_r, qr_s, qr_r,
    gdS, grS, gdA, grA, c0S, c0A, stS, PD, PR, sem,
):
    px = lax.axis_index("px")
    py = lax.axis_index("py")
    half = n_py // 2
    h0 = py // half
    q0 = py % half
    px_next, px_prev = (px + 1) % n_px, (px + n_px - 1) % n_px
    py_next, py_prev = (py + 1) % n_py, (py + n_py - 1) % n_py

    def remote(src, dst, s, r, to):
        return pltpu.make_async_remote_copy(
            src, dst, sem.at[s], sem.at[r], device_id=to, device_id_type=MESH
        )

    def wait_bytes(view, s):
        pltpu.make_async_copy(view, view, sem.at[s]).wait()

    load_b = pltpu.make_async_copy(loads, R, sem.at[L_B])
    load_t = pltpu.make_async_copy(targets, T, sem.at[L_T])
    load_b.start()
    load_t.start()

    barrier = pltpu.get_barrier_semaphore()
    for i in range(1, n_py):
        pl.semaphore_signal(barrier, inc=1, device_id=(px, (py + i) % n_py), device_id_type=MESH)
    pl.semaphore_signal(barrier, inc=1, device_id=(px_next, py), device_id_type=MESH)
    pl.semaphore_signal(barrier, inc=1, device_id=(px_prev, py), device_id_type=MESH)

    live = iota((1, 128), 1) < count[0, 0]
    q_live = jnp.where(live, cab_q[...], 0.0)
    row8 = iota((8, 128), 0)
    cab_s[...] = jnp.where(
        row8 == 0,
        cab_a[...].astype(F32),
        jnp.where(row8 == 1, cab_b[...].astype(F32), jnp.where(row8 == 2, q_live, 0.0)),
    )
    m_id = iota((128, 128), 0)
    code = (m_id // 8 * 4 + m_id % 4).astype(F32)
    m_half = m_id % 8 // 4

    def ends(values, which):
        mine = m_half == which
        at_a = jnp.where(mine & (code == values[0:1]), 1.0, 0.0)
        at_b = jnp.where(mine & (code == values[1:2]), 1.0, 0.0)
        return at_a, at_b

    at_a, at_b = ends(cab_s[...], h0)
    slot_q = jnp.sum((at_a + at_b) * q_live, axis=1, keepdims=True)
    dq_s[...] = jnp.broadcast_to(slot_q, (128, 128)).reshape(n_py, 8, 128)
    qd_s[...] = jnp.concatenate(
        [jnp.broadcast_to(q_down[TX - 1 : TX, :], (8, TY)), jnp.zeros((8, 128 - TY), F32)], axis=1
    )
    qr_s[...] = jnp.concatenate([q_right[...], jnp.zeros((TX, 128 - TY), F32)], axis=1)

    pl.semaphore_wait(barrier, n_py + 1)

    for i in range(1, n_py):
        t = (py + i) % n_py
        remote(dq_s.at[t], dq_r.at[py], S_DQ, R_DQ, (px, t)).start()
    cab_copy = remote(cab_s, cab_r, S_CAB, R_CAB, (px, (py + half) % n_py))
    qd_copy = remote(qd_s, qd_r, S_QD, R_QD, (px_next, py))
    qr_copy = remote(qr_s, qr_r, S_QR, R_QR, (px, py_next))
    cab_copy.start()
    qd_copy.start()
    qr_copy.start()
    dq_r[py] = dq_s[py]

    p_id, l_id = iota((SLOTS, 3 * SLOTS), 0), iota((SLOTS, 3 * SLOTS), 1) % SLOTS
    perm = jnp.where(p_id == (l_id // 8 + half * (l_id % 8 // 4)) * 4 + l_id % 4, 1.0, 0.0)
    row_f = jnp.broadcast_to(rows_v[...].astype(F32), (8, SLOTS))
    in_lanes = jnp.dot(row_f, perm, precision=HIGHEST, preferred_element_type=F32)[0:1]
    in_rows = lax.dot_general(
        perm[:, :SLOTS], row_f, (((0,), (1,)), ((), ())), precision=HIGHEST, preferred_element_type=F32
    )[:, 0:1]
    C3[...] = jnp.where(
        jnp.broadcast_to(in_rows, (SLOTS, 3 * SLOTS)) == in_lanes, 1.0, 0.0
    ).astype(BF16)

    def one_hot(i, carry):
        node = (iota((TY, 3 * SLOTS), 0) + i * TY).astype(F32)
        ONE[pl.ds(pl.multiple_of(i * TY, TY), TY)] = jnp.where(node == in_lanes, 1.0, 0.0).astype(BF16)
        return carry

    lax.fori_loop(0, TX, one_hot, 0)

    qd_copy.wait()
    qr_copy.wait()
    gi = iota((TX, TY), 0) + px * TX
    gj = iota((TX, TY), 1) + py * TY
    w_down = jnp.where(gi < n_px * TX - 1, q_down[...], 0.0)
    w_right = jnp.where(gj < n_py * TY - 1, q_right[...], 0.0)
    prev_down = jnp.where(px > 0, qd_r[0:1, :TY], 0.0)
    prev_right = jnp.where(py > 0, qr_r[:, TY - 1 : TY], 0.0)
    w_up = jnp.concatenate([prev_down, w_down[:-1]], 0)
    w_left = jnp.concatenate([prev_right, w_right[:, :-1]], 1)
    diag = anchor[...] + w_down + w_up + w_right + w_left
    stacked = jnp.concatenate(
        [diag, w_down, w_right, w_left, jnp.broadcast_to(prev_down, (8, TY))], 0
    )
    eye = jnp.where(iota((TY, TY), 0) == iota((TY, TY), 1), 1.0, 0.0)
    columns = dot_t(eye, stacked, HIGHEST)

    def spread(col):
        return jnp.broadcast_to(columns[:, col : col + 1], (TY, V))

    WD[0:TY] = spread(4 * TX)
    for i in range(TX):
        at = pl.ds(i * TY, TY)
        GD[at] = spread(i)
        WD[pl.ds((i + 1) * TY, TY)] = spread(TX + i)
        WR[at] = spread(2 * TX + i)
        WL[at] = spread(3 * TX + i)

    cab_copy.wait()
    pa, pb = ends(cab_r[...], 1 - h0)
    inc_own, inc_other = at_a - at_b, pa - pb
    LM[...] = dot_t(inc_own * q_live, inc_own, HIGHEST) + dot_t(
        inc_other * cab_r[2:3], inc_other, HIGHEST
    )
    mine_rows = LM[pl.ds(pl.multiple_of(h0 * SLOTS, SLOTS), SLOTS)]
    l_high, l_low = split2(mine_rows)
    LH[:, 0:128] = l_high
    LH[:, 128:256] = l_high
    LL[...] = l_low

    wait_bytes(dq_r.at[pl.ds(0, n_py - 1)], R_DQ)
    slot_sum = (dq_r[0:half] + dq_r[half:]).reshape(SLOTS, V)
    LD = dot(ONE[...], jnp.concatenate(split3(slot_sum), 0))
    INV[...] = 1.0 / (GD[...] + LD)
    wait_bytes(dq_s.at[pl.ds(0, n_py - 1)], S_DQ)

    def gather(src, dst):
        def rows_of(w, carry):
            for e in range(8):
                node = rows_s[0, (w + half * (e // 4)) * 4 + e % 4]
                for c in range(3):
                    dst[c, pl.ds(w * 8 + e, 1), :] = src[c, pl.ds(node, 1), :]
            return carry

        lax.fori_loop(0, half, rows_of, 0)

    def gather_inv(w, carry):
        for e in range(8):
            node = rows_s[0, (w + half * (e // 4)) * 4 + e % 4]
            inv_l[pl.ds(w * 8 + e, 1), :] = INV[pl.ds(node, 1), :]
        return carry

    lax.fori_loop(0, half, gather_inv, 0)

    def send_lent(src, dst, s, r):
        for i in range(1, n_py):
            t = (py + i) % n_py
            remote(src.at[t % half], dst.at[py], s, r, (px, t)).start()
        dst[py] = src[q0]

    def put(dst, c, value):
        dst[:, c] = value.reshape(half, 8, V)

    load_b.wait()
    gather(R, rg_l)
    for c in range(3):
        first = inv_l[...] * rg_l[c] * (1.0 / THETA)
        d_l[c] = first
        x_l[c] = first
        put(Y, c, first)
    send_lent(Y, recv1.at[0], S_P1, R_P1)
    load_t.wait()
    gather(T, t_l)

    last = 2 * ROUNDS
    save_shape = pltpu.make_async_copy(S, shape_out, sem.at[L_S])
    shape_down = remote(S.at[:, pl.ds(0, TY)], gdS, S_GD, R_GD, (px_prev, py))
    shape_right = remote(c0S, grS, S_GR, R_GR, (px, py_prev))

    def spans(i):
        return pl.ds(pl.multiple_of(i * TY, TY), TY)

    def scatter(lo, hi):
        SF[lo * TY : hi * TY] = dot(ONE[lo * TY : hi * TY], F3[...])

    def advance(i, a, b):
        at = spans(i)
        inv = INV[at] * b
        for c in range(3):
            r = R[c, at] - SF[at, c * V : (c + 1) * V]
            R[c, at] = r
            d = a * D[c, at] + inv * r
            D[c, at] = d
            X[c, at] = X[c, at] + d

    def begin(i):
        at = spans(i)
        inv = INV[at] * (1.0 / THETA)
        for c in range(3):
            d = inv * R[c, at]
            D[c, at] = d
            X[c, at] = d

    def turn(i, a, b):
        at = spans(i)
        inv = INV[at]
        for c in range(3):
            r = R[c, at] - SF[at, c * V : (c + 1) * V]
            x = X[c, at] + (a * D[c, at] + (inv * b) * r)
            S[c, at] = x
            r = x - T[c, at]
            R[c, at] = r
            d = inv * r * (1.0 / THETA)
            D[c, at] = d
            X[c, at] = d

    def each(fn, lo, hi):
        def body(i, carry):
            fn(i)
            return carry

        lax.fori_loop(lo, hi, body, 0)

    def stencil(i, par, above, below):
        at = spans(i)
        gd, wu, wd, wr, wl = GD[at], WD[at], WD[spans(i + 1)], WR[at], WL[at]
        row = iota((TY, V), 0)
        for c in range(3):
            d = D[c, at]
            left = jnp.where(row == 0, lf[par, c, pl.ds(i, 1), :], pltpu.roll(d, 1, 0))
            right = jnp.where(row == TY - 1, rt[par, c, pl.ds(i, 1), :], pltpu.roll(d, TY - 1, 0))
            near = wu * above(c) + wd * below(c) + wl * left + wr * right
            R[c, at] = R[c, at] - (gd * d - near)

    def round_(t, carry):
        par = t % 2
        first, middle = t == 0, t == ROUNDS
        usual = jnp.logical_and(t != 0, t != ROUNDS)
        a_prev, b_prev = coef_of((t + ROUNDS - 1) % ROUNDS)
        a_next, b_next = coef_of(t % ROUNDS)

        @pl.when(t != 0)
        def _():
            scatter(0, 1)
            scatter(TX - 1, TX)

        @pl.when(first)
        def _():
            begin(0)
            begin(TX - 1)

        @pl.when(usual)
        def _():
            advance(0, a_prev, b_prev)
            advance(TX - 1, a_prev, b_prev)

        @pl.when(middle)
        def _():
            turn(0, a_prev, b_prev)
            turn(TX - 1, a_prev, b_prev)

        to_next = remote(
            D.at[:, pl.ds((TX - 1) * TY, TY)], up.at[par], S_UP, R_UP + par, (px_next, py)
        )
        to_prev = remote(D.at[:, pl.ds(0, TY)], dn.at[par], S_DN, R_DN + par, (px_prev, py))
        to_next.start()
        to_prev.start()

        @pl.when(t != 0)
        def _():
            scatter(1, TX - 1)

        @pl.when(first)
        def _():
            each(begin, 1, TX - 1)

        @pl.when(usual)
        def _():
            each(lambda i: advance(i, a_prev, b_prev), 1, TX - 1)

        @pl.when(middle)
        def _():
            each(lambda i: turn(i, a_prev, b_prev), 1, TX - 1)

        for c in range(3):
            for i in range(TX):
                cl[c, i : i + 1] = D[c, i * TY : i * TY + 1]
                cr[c, i : i + 1] = D[c, (i + 1) * TY - 1 : (i + 1) * TY]
        to_right = remote(cr, lf.at[par], S_LF, R_LF + par, (px, py_next))
        to_left = remote(cl, rt.at[par], S_RT, R_RT + par, (px, py_prev))
        to_right.start()
        to_left.start()

        @pl.when(middle)
        def _():
            for c in range(3):
                for i in range(TX):
                    c0S[c, i : i + 1] = S[c, i * TY : i * TY + 1]
            save_shape.start()
            shape_down.start()
            shape_right.start()

        wait_bytes(recv1.at[0, pl.ds(0, n_py - 1)], R_P1 + par)
        for c in range(3):
            high, low = split2(recv1[par, :, c].reshape(128, V))
            force = dot(LH[...], jnp.concatenate([high, low], 0)) + dot(LL[...], high)
            put(Fs, c, force)
        for i in range(1, half):
            q = (q0 + i) % half
            remote(Fs.at[q], frecv.at[q0], S_P2, R_P2, (px, h0 * half + q)).start()
        frecv[q0] = Fs[q0]

        to_right.wait()
        to_left.wait()
        each(
            lambda i: stencil(
                i, par, lambda c: D[c, spans(i - 1)], lambda c: D[c, spans(i + 1)]
            ),
            1,
            TX - 1,
        )
        to_next.wait()
        to_prev.wait()
        stencil(0, par, lambda c: up[par, c], lambda c: D[c, spans(1)])
        stencil(TX - 1, par, lambda c: D[c, spans(TX - 2)], lambda c: dn[par, c])
        gather(R, rg_l)
        wait_bytes(recv1.at[0, pl.ds(0, n_py - 1)], S_P1)

        wait_bytes(frecv.at[pl.ds(0, half - 1)], R_P2)
        for c in range(3):
            high, mid, low = split3(frecv[:, c].reshape(SLOTS, V))
            lanes = pl.ds(c * V, V)
            F3[0:SLOTS, lanes] = high
            F3[SLOTS : 2 * SLOTS, lanes] = mid
            F3[2 * SLOTS :, lanes] = low
        at_node = dot(C3[...], F3[...])
        for c in range(3):
            r = rg_l[c] - at_node[:, c * V : (c + 1) * V]
            d = a_next * d_l[c] + (b_next * inv_l[...]) * r
            d_l[c] = d
            x_l[c] = x_l[c] + d
            put(Y, c, d)

        @pl.when(t == ROUNDS - 1)
        def _():
            for c in range(3):
                put(XS, c, x_l[c])
                d = inv_l[...] * (x_l[c] - t_l[c]) * (1.0 / THETA)
                d_l[c] = d
                x_l[c] = d
                put(Y, c, d)

        @pl.when(t == last - 1)
        def _():
            for c in range(3):
                put(Y, c, x_l[c])

        send_lent(Y, recv1.at[1 - par], S_P1, R_P1 + 1 - par)

        @pl.when(t == ROUNDS - 1)
        def _():
            send_lent(XS, recvS, S_SH, R_SH)

        wait_bytes(frecv.at[pl.ds(0, half - 1)], S_P2)
        return carry

    lax.fori_loop(0, last, round_, 0)

    a, b = COEF[-1]
    scatter(0, TX)
    each(lambda i: advance(i, a, b), 0, TX)
    for c in range(3):
        for i in range(TX):
            c0A[c, i : i + 1] = X[c, i * TY : i * TY + 1]
    adjoint_down = remote(X.at[:, pl.ds(0, TY)], gdA, S_HD, R_HD, (px_prev, py))
    adjoint_right = remote(c0A, grA, S_HR, R_HR, (px, py_prev))
    adjoint_down.start()
    adjoint_right.start()
    save_adjoint = pltpu.make_async_copy(X, adjoint_out, sem.at[L_A])
    save_adjoint.start()


    def stretches(view, store):
        at_a_, at_b_ = ends(cab_s[...], h0)
        inc_ = (at_a_ - at_b_).astype(BF16)
        total = None
        for c in range(3):
            out = None
            for part in split3(view[:, c].reshape(128, V)):
                piece = lax.dot_general(
                    inc_, part, (((0,), (0,)), ((), ())), preferred_element_type=F32
                )
                out = piece if out is None else out + piece
            if store:
                stS[c] = out
            else:
                term = out * stS[c]
                total = term if total is None else total + term
        return total

    def lane_sums(values):
        ones = jnp.ones((8, V), BF16)
        out = None
        for part in split3(values):
            piece = dot_t(ones, part)
            out = piece if out is None else out + piece
        return out[0:1] * (-1.0 / V)

    wait_bytes(recvS.at[pl.ds(0, n_py - 1)], R_SH)
    wait_bytes(recvS.at[pl.ds(0, n_py - 1)], S_SH)
    stretches(recvS, True)
    shape_down.wait()
    shape_right.wait()

    def down(i, below_s, below_a):
        at = spans(i)
        total = None
        for c in range(3):
            term = (X[c, at] - below_a(c)) * (S[c, at] - below_s(c))
            total = term if total is None else total + term
        PD[at] = total

    each(
        lambda i: down(i, lambda c: S[c, spans(i + 1)], lambda c: X[c, spans(i + 1)]), 0, TX - 1
    )
    adjoint_right.wait()

    def beside(i):
        at = spans(i)
        row = iota((TY, V), 0)
        total = None
        for c in range(3):
            s, x = S[c, at], X[c, at]
            s_next = jnp.where(row == TY - 1, grS[c, pl.ds(i, 1), :], pltpu.roll(s, TY - 1, 0))
            x_next = jnp.where(row == TY - 1, grA[c, pl.ds(i, 1), :], pltpu.roll(x, TY - 1, 0))
            term = (x - x_next) * (s - s_next)
            total = term if total is None else total + term
        PR[at] = total

    each(beside, 0, TX)
    right_sums = lane_sums(PR[...])
    adjoint_down.wait()
    down(TX - 1, lambda c: gdS[c], lambda c: gdA[c])
    down_sums = lane_sums(PD[...])
    for i in range(TX):
        lanes = slice(i * TY, (i + 1) * TY)
        down_out[i : i + 1] = down_sums[:, lanes]
        right_out[i : i + 1] = right_sums[:, lanes]
    down_out[...] = jnp.where(gi < n_px * TX - 1, down_out[...], 0.0)
    right_out[...] = jnp.where(gj < n_py * TY - 1, right_out[...], 0.0)

    par = last % 2
    wait_bytes(recv1.at[0, pl.ds(0, n_py - 1)], R_P1 + par)
    long_sums = lane_sums(stretches(recv1.at[par], False))
    long_out[...] = jnp.where(live, long_sums, 0.0)
    wait_bytes(recv1.at[0, pl.ds(0, n_py - 1)], S_P1)
    save_shape.wait()
    save_adjoint.wait()


def per_device(
    n_px, n_py,
    loads, targets, anchor, q_down, q_right, send_rows, cable_a, cable_b, cable_count, cable_q,
):
    half = n_py // 2
    field = (3, NODES, V)
    vmem = pl.BlockSpec(memory_space=pltpu.VMEM)
    smem = pl.BlockSpec(memory_space=pltpu.SMEM)
    anywhere = pl.BlockSpec(memory_space=pl.ANY)

    def scratch(*shape, dtype=F32):
        return pltpu.VMEM(shape, dtype)

    lent = (half, 3, 8, V)
    shape_field, adjoint_field, grad_down, grad_right, grad_long = pl.pallas_call(
        functools.partial(kernel, n_px, n_py),
        out_shape=(
            jax.ShapeDtypeStruct(field, F32),
            jax.ShapeDtypeStruct(field, F32),
            jax.ShapeDtypeStruct((TX, TY), F32),
            jax.ShapeDtypeStruct((TX, TY), F32),
            jax.ShapeDtypeStruct((1, 128), F32),
        ),
        in_specs=[anywhere, anywhere, vmem, vmem, vmem, smem, vmem, vmem, vmem, smem, vmem],
        out_specs=(anywhere, anywhere, vmem, vmem, vmem),
        scratch_shapes=[
            scratch(*field),
            scratch(*field),
            scratch(*field),
            scratch(*field),
            scratch(*field),
            scratch(NODES, 3 * V),
            scratch(NODES, V),
            scratch(NODES + TY, V),
            scratch(NODES, V),
            scratch(NODES, V),
            scratch(NODES, V),
            scratch(NODES, 3 * SLOTS, dtype=BF16),
            scratch(3 * SLOTS, 3 * V, dtype=BF16),
            scratch(SLOTS, 3 * SLOTS, dtype=BF16),
            scratch(SLOTS, 256, dtype=BF16),
            scratch(SLOTS, 128, dtype=BF16),
            scratch(128, 128),
            scratch(3, SLOTS, V),
            scratch(3, SLOTS, V),
            scratch(3, SLOTS, V),
            scratch(3, SLOTS, V),
            scratch(SLOTS, V),
            scratch(*lent),
            scratch(*lent),
            scratch(2, n_py, 3, 8, V),
            scratch(n_py, 3, 8, V),
            scratch(*lent),
            scratch(*lent),
            scratch(2, 3, TY, V),
            scratch(2, 3, TY, V),
            scratch(2, 3, TX, V),
            scratch(2, 3, TX, V),
            scratch(3, TX, V),
            scratch(3, TX, V),
            scratch(8, 128),
            scratch(8, 128),
            scratch(n_py, 8, 128),
            scratch(n_py, 8, 128),
            scratch(8, 128),
            scratch(8, 128),
            scratch(TX, 128),
            scratch(TX, 128),
            scratch(3, TY, V),
            scratch(3, TX, V),
            scratch(3, TY, V),
            scratch(3, TX, V),
            scratch(3, TX, V),
            scratch(3, TX, V),
            scratch(3, 128, V),
            scratch(NODES, V),
            scratch(NODES, V),
            pltpu.SemaphoreType.DMA((N_SEM,)),
        ],
        compiler_params=pltpu.CompilerParams(
            collective_id=0, has_side_effects=True, vmem_limit_bytes=40 << 20
        ),
        name="cable_net",
    )(
        loads.reshape(field),
        targets.reshape(field),
        anchor,
        q_down,
        q_right,
        send_rows,
        send_rows,
        cable_a,
        cable_b,
        cable_count,
        cable_q,
    )
    tile = (3, TX, TY, V)
    return shape_field.reshape(tile), adjoint_field.reshape(tile), grad_down, grad_right, grad_long


def solution(mesh):
    field = P(None, "px", "py", None)
    flat = P("px", "py")
    return jax.shard_map(
        functools.partial(per_device, mesh.shape["px"], mesh.shape["py"]),
        mesh=mesh,
        in_specs=(field, field) + (flat,) * 8,
        out_specs=(field, field, flat, flat, flat),
        check_vma=False,
    )
```

```python
import functools

import jax
import jax.numpy as jnp
from jax import lax
from jax.experimental import pallas as pl
from jax.experimental.pallas import tpu as pltpu
from jax.sharding import PartitionSpec as P

MESH = pl.DeviceIdType.MESH
F32 = jnp.float32
BF16 = jnp.bfloat16
HIGHEST = lax.Precision.HIGHEST

STEPS = 7
ROUNDS = STEPS - 1
TX, TY, V = 16, 64, 128
NODES = TX * TY
SLOTS = 64
LOW, HIGH = 0.05, 2.0
LIMIT = 60 << 20
THETA = (HIGH + LOW) / 2.0
DELTA = (HIGH - LOW) / 2.0


def coefficients():
    sigma = THETA / DELTA
    rho = 1.0 / sigma
    pairs = []
    for _ in range(ROUNDS):
        rho_new = 1.0 / (2.0 * sigma - rho)
        pairs.append((rho_new * rho, 2.0 * rho_new / DELTA))
        rho = rho_new
    return pairs


COEF = coefficients()


def coef_of(round_):
    a, b = (jnp.float32(value) for value in COEF[-1])
    for k in range(ROUNDS - 1):
        a = jnp.where(round_ == k, jnp.float32(COEF[k][0]), a)
        b = jnp.where(round_ == k, jnp.float32(COEF[k][1]), b)
    return a, b


def split2(x):
    high = x.astype(BF16)
    return high, (x - high.astype(F32)).astype(BF16)


def split3(x):
    high = x.astype(BF16)
    rest = x - high.astype(F32)
    mid = rest.astype(BF16)
    return high, mid, (rest - mid.astype(F32)).astype(BF16)


def dot(a, b):
    return jnp.dot(a, b, preferred_element_type=F32)


def dot_t(a, b, precision=None):
    return lax.dot_general(
        a, b, (((1,), (1,)), ((), ())), precision=precision, preferred_element_type=F32
    )


def iota(shape, dim):
    return lax.broadcasted_iota(jnp.int32, shape, dim)


(
    S_P1, R_P1, S_P2, R_P2, S_UP, R_UP, S_DN, R_DN, S_LF, R_LF, S_RT, R_RT,
    S_CAB, R_CAB, S_DQ, R_DQ, S_QD, R_QD, S_QR, R_QR, S_SH, R_SH, S_AD, R_AD,
    S_GD, R_GD, S_GR, R_GR, S_HD, R_HD, S_HR, R_HR, L_B, L_T, L_S, L_A,
    L_0, L_1, L_2, L_3, L_4, L_5, L_6, L_7,
) = range(0, 88, 2)
N_SEM = 88


def kernel(
    n_px, n_py,
    loads, targets, anchor_h, q_down_h, q_right_h, rows_s, rows_h, cab_a_h, cab_b_h, count, cab_q_h,
    shape_out, adjoint_out, down_out, right_out, long_out,
    R, D, X, S, T, SF, GD, WD, WR, WL, INV, ONE, F2, CR, L3, IO, IP,
    rg_l, d_l, x_l, t_l, inv_l, Y, XS, recv1, recvS, recvA, Fs, frecv,
    up, dn, lf, rt, cl, cr, cab_s, cab_r, dq_s, dq_r, qd_s, qd_r, qr_s, qr_r,
    gdS, grS, gdA, grA, c0S, c0A, stS, PD, PR,
    anchor, q_down, q_right, rows_v, cab_a, cab_b, cab_q, sem,
):
    px = lax.axis_index("px")
    py = lax.axis_index("py")
    half = n_py // 2
    h0 = py // half
    q0 = py % half
    px_next, px_prev = (px + 1) % n_px, (px + n_px - 1) % n_px
    py_next, py_prev = (py + 1) % n_py, (py + n_py - 1) % n_py

    def remote(src, dst, s, r, to):
        return pltpu.make_async_remote_copy(
            src, dst, sem.at[s], sem.at[r], device_id=to, device_id_type=MESH
        )

    def wait_bytes(view, s):
        pltpu.make_async_copy(view, view, sem.at[s]).wait()

    load_b = pltpu.make_async_copy(loads, R, sem.at[L_B])
    load_t = pltpu.make_async_copy(targets, T, sem.at[L_T])
    small = [
        pltpu.make_async_copy(src, dst, sem.at[s])
        for src, dst, s in (
            (cab_a_h, cab_a, L_0), (cab_b_h, cab_b, L_1),
            (cab_q_h, cab_q, L_3), (q_down_h, q_down, L_4), (q_right_h, q_right, L_5),
            (rows_h, rows_v, L_6), (anchor_h, anchor, L_7),
        )
    ]
    for copy in small:
        copy.start()
    load_b.start()
    load_t.start()

    barrier = pltpu.get_barrier_semaphore()
    for i in range(1, n_py):
        pl.semaphore_signal(barrier, inc=1, device_id=(px, (py + i) % n_py), device_id_type=MESH)
    pl.semaphore_signal(barrier, inc=1, device_id=(px_next, py), device_id_type=MESH)
    pl.semaphore_signal(barrier, inc=1, device_id=(px_prev, py), device_id_type=MESH)

    wide = half // 2
    y0, c0 = q0 // 2, q0 % 2
    order = sorted(
        (v for v in ((dx, dy, dc) for dx in (0, 1) for dy in range(wide) for dc in (0, 1)) if any(v)),
        key=lambda v: -(2 * v[0] + min(v[1], wide - v[1])),
    )

    def other(dx, dy, dc):
        return (h0 + dx) % 2, (y0 + dy) % wide * 2 + (c0 + dc) % 2

    peers = [other(*v) for v in order]
    near_peers = [other(*v) for v in order if v[0] == 0]

    for copy in small:
        copy.wait()

    live = iota((1, 128), 1) < count[0, 0]
    q_live = jnp.where(live, cab_q[...], 0.0)
    row8 = iota((8, 128), 0)
    cab_s[...] = jnp.where(
        row8 == 0,
        cab_a[...].astype(F32),
        jnp.where(row8 == 1, cab_b[...].astype(F32), jnp.where(row8 == 2, q_live, 0.0)),
    )
    m_id = iota((128, 128), 0)
    code = (m_id // 8 * 4 + m_id % 4).astype(F32)
    m_half = m_id % 8 // 4

    def ends(values, which):
        mine = m_half == which
        at_a = jnp.where(mine & (code == values[0:1]), 1.0, 0.0)
        at_b = jnp.where(mine & (code == values[1:2]), 1.0, 0.0)
        return at_a, at_b

    at_a, at_b = ends(cab_s[...], h0)
    slot_q = jnp.sum((at_a + at_b) * q_live, axis=1, keepdims=True)
    dq_s[...] = jnp.broadcast_to(slot_q, (128, 128)).reshape(n_py, 8, 128)
    qd_s[...] = jnp.concatenate(
        [jnp.broadcast_to(q_down[TX - 1 : TX, :], (8, TY)), jnp.zeros((8, 128 - TY), F32)], axis=1
    )
    qr_s[...] = jnp.concatenate([q_right[...], jnp.zeros((TX, 128 - TY), F32)], axis=1)

    p_id, l_id = iota((SLOTS, 2 * SLOTS), 0), iota((SLOTS, 2 * SLOTS), 1) % SLOTS
    perm = jnp.where(p_id == (l_id // 8 + half * (l_id % 8 // 4)) * 4 + l_id % 4, 1.0, 0.0)
    row_f = jnp.broadcast_to(rows_v[...].astype(F32), (8, SLOTS))
    in_lanes = jnp.dot(row_f, perm, precision=HIGHEST, preferred_element_type=F32)[0:1]
    in_rows = lax.dot_general(
        perm[:, :SLOTS], row_f, (((0,), (1,)), ((), ())), precision=HIGHEST, preferred_element_type=F32
    )[:, 0:1]
    CR[0:SLOTS] = jnp.where(
        jnp.broadcast_to(in_rows, (SLOTS, 2 * SLOTS)) == in_lanes, 1.0, 0.0
    ).astype(BF16)

    def one_hot(i, carry):
        node = (iota((TY, 2 * SLOTS), 0) + i * TY).astype(F32)
        ONE[pl.ds(pl.multiple_of(i * TY, TY), TY)] = jnp.where(node == in_lanes, 1.0, 0.0).astype(BF16)
        return carry

    lax.fori_loop(0, TX, one_hot, 0)
    CR[SLOTS : SLOTS + TY] = ONE[0:TY]
    CR[SLOTS + TY :] = ONE[NODES - TY :]

    pl.semaphore_wait(barrier, n_py + 1)

    for h, q in peers:
        t = h * half + q
        remote(dq_s.at[t], dq_r.at[py], S_DQ, R_DQ, (px, t)).start()
    cab_copy = remote(cab_s, cab_r, S_CAB, R_CAB, (px, (py + half) % n_py))
    qd_copy = remote(qd_s, qd_r, S_QD, R_QD, (px_next, py))
    qr_copy = remote(qr_s, qr_r, S_QR, R_QR, (px, py_next))
    cab_copy.start()
    qd_copy.start()
    qr_copy.start()
    dq_r[py] = dq_s[py]

    qd_copy.wait()
    qr_copy.wait()
    gi = iota((TX, TY), 0) + px * TX
    gj = iota((TX, TY), 1) + py * TY
    w_down = jnp.where(gi < n_px * TX - 1, q_down[...], 0.0)
    w_right = jnp.where(gj < n_py * TY - 1, q_right[...], 0.0)
    prev_down = jnp.where(px > 0, qd_r[0:1, :TY], 0.0)
    prev_right = jnp.where(py > 0, qr_r[:, TY - 1 : TY], 0.0)
    w_up = jnp.concatenate([prev_down, w_down[:-1]], 0)
    w_left = jnp.concatenate([prev_right, w_right[:, :-1]], 1)
    diag = anchor[...] + w_down + w_up + w_right + w_left
    stacked = jnp.concatenate(
        [diag, w_down, w_right, w_left, jnp.broadcast_to(prev_down, (8, TY))], 0
    )
    eye = jnp.where(iota((TY, TY), 0) == iota((TY, TY), 1), 1.0, 0.0)
    columns = dot_t(eye, stacked, HIGHEST)

    def spread(col):
        return jnp.broadcast_to(columns[:, col : col + 1], (TY, V))

    WD[0:TY] = spread(4 * TX)
    for i in range(TX):
        at = pl.ds(i * TY, TY)
        GD[at] = spread(i)
        WD[pl.ds((i + 1) * TY, TY)] = spread(TX + i)
        WR[at] = spread(2 * TX + i)
        WL[at] = spread(3 * TX + i)

    cab_copy.wait()
    pa, pb = ends(cab_r[...], 1 - h0)
    inc_own, inc_other = at_a - at_b, pa - pb
    IO[...] = inc_own
    IP[...] = inc_other
    of_half = pl.ds(pl.multiple_of(h0 * SLOTS, SLOTS), SLOTS)
    matrix = dot_t(inc_own * q_live, IO[of_half], HIGHEST) + dot_t(
        inc_other * cab_r[2:3], IP[of_half], HIGHEST
    )
    L3[...] = jnp.concatenate([matrix, matrix - matrix.astype(BF16).astype(F32)], 1).astype(BF16)

    def gather(src, dst):
        def rows_of(w, carry):
            for e in range(8):
                node = rows_s[0, (w + half * (e // 4)) * 4 + e % 4]
                for c in range(3):
                    dst[c, pl.ds(w * 8 + e, 1), :] = src[c, pl.ds(node, 1), :]
            return carry

        lax.fori_loop(0, half, rows_of, 0)

    def gather_diag(w, carry):
        for e in range(8):
            node = rows_s[0, (w + half * (e // 4)) * 4 + e % 4]
            inv_l[pl.ds(w * 8 + e, 1), :] = GD[pl.ds(node, 1), :]
        return carry

    def send_all(src, dst, s, r):
        for h, q in peers:
            remote(src.at[q], dst.at[py], s, r, (px, h * half + q)).start()
        dst[py] = src[q0]

    def send_lent():
        for h, q in near_peers:
            remote(Y.at[q], recv1.at[q0], S_P1, R_P1, (px, h * half + q)).start()
        recv1[q0] = Y[q0]

    def put(dst, c, value):
        dst[:, c] = value.reshape(dst.shape[0], 8, V)

    lax.fori_loop(0, half, gather_diag, 0)
    load_b.wait()
    gather(R, rg_l)

    wait_bytes(dq_r.at[pl.ds(0, n_py - 1)], R_DQ)
    slot_sum = (dq_r[0:half] + dq_r[half:]).reshape(SLOTS, V)
    slot_sum = jnp.concatenate(split2(slot_sum), 0)
    inv_l[...] = 1.0 / (inv_l[...] + dot(CR[0:SLOTS], slot_sum))
    for c in range(3):
        first = inv_l[...] * rg_l[c] * (1.0 / THETA)
        d_l[c] = first
        x_l[c] = first
        put(Y, c, first)
    send_lent()
    INV[...] = 1.0 / (GD[...] + dot(ONE[...], slot_sum))

    last = 2 * ROUNDS
    save_shape = pltpu.make_async_copy(S, shape_out, sem.at[L_S])
    shape_down = remote(S.at[:, pl.ds(0, TY)], gdS, S_GD, R_GD, (px_prev, py))
    shape_right = remote(c0S, grS, S_GR, R_GR, (px, py_prev))

    def spans(i):
        return pl.ds(pl.multiple_of(i * TY, TY), TY)

    def scatter(lo, hi):
        SF[lo * TY : hi * TY] = dot(ONE[lo * TY : hi * TY], F2[...])

    def advance(i, a, b):
        at = spans(i)
        inv = INV[at] * b
        for c in range(3):
            r = R[c, at] - SF[at, c * V : (c + 1) * V]
            R[c, at] = r
            d = a * D[c, at] + inv * r
            D[c, at] = d
            X[c, at] = X[c, at] + d

    def begin(i):
        at = spans(i)
        inv = INV[at] * (1.0 / THETA)
        for c in range(3):
            d = inv * R[c, at]
            D[c, at] = d
            X[c, at] = d

    def turn(i, a, b):
        at = spans(i)
        inv = INV[at]
        for c in range(3):
            r = R[c, at] - SF[at, c * V : (c + 1) * V]
            x = X[c, at] + (a * D[c, at] + (inv * b) * r)
            S[c, at] = x
            r = x - T[c, at]
            R[c, at] = r
            d = inv * r * (1.0 / THETA)
            D[c, at] = d
            X[c, at] = d

    def each(fn, lo, hi):
        def body(i, carry):
            fn(i)
            return carry

        lax.fori_loop(lo, hi, body, 0)

    def stencil(i, par, above, below):
        at = spans(i)
        gd, wu, wd, wr, wl = GD[at], WD[at], WD[spans(i + 1)], WR[at], WL[at]
        row = iota((TY, V), 0)
        for c in range(3):
            d = D[c, at]
            left = jnp.where(row == 0, lf[par, c, pl.ds(i, 1), :], pltpu.roll(d, 1, 0))
            right = jnp.where(row == TY - 1, rt[par, c, pl.ds(i, 1), :], pltpu.roll(d, TY - 1, 0))
            near = wu * above(c) + wd * below(c) + wl * left + wr * right
            R[c, at] = R[c, at] - (gd * d - near)

    def stretches(view, store):
        at_a_, at_b_ = ends(cab_s[...], h0)
        inc_ = (at_a_ - at_b_).astype(BF16)
        total = None
        for c in range(3):
            out = None
            for part in split3(view[:, c].reshape(128, V)):
                piece = lax.dot_general(
                    inc_, part, (((0,), (0,)), ((), ())), preferred_element_type=F32
                )
                out = piece if out is None else out + piece
            if store:
                stS[c] = out
            else:
                term = out * stS[c]
                total = term if total is None else total + term
        return total

    def round_(t, carry):
        par = t % 2
        first, middle = t == 0, t == ROUNDS
        usual = jnp.logical_and(t != 0, t != ROUNDS)
        a_prev, b_prev = coef_of((t + ROUNDS - 1) % ROUNDS)
        a_next, b_next = coef_of(t % ROUNDS)

        @pl.when(first)
        def _():
            begin(0)
            begin(TX - 1)

        @pl.when(usual)
        def _():
            advance(0, a_prev, b_prev)
            advance(TX - 1, a_prev, b_prev)

        @pl.when(middle)
        def _():
            turn(0, a_prev, b_prev)
            turn(TX - 1, a_prev, b_prev)

        to_next = remote(
            D.at[:, pl.ds((TX - 1) * TY, TY)], up.at[par], S_UP, R_UP + par, (px_next, py)
        )
        to_prev = remote(D.at[:, pl.ds(0, TY)], dn.at[par], S_DN, R_DN + par, (px_prev, py))
        to_next.start()
        to_prev.start()

        @pl.when(t != 0)
        def _():
            scatter(1, TX - 1)

        @pl.when(first)
        def _():
            each(begin, 1, TX - 1)

        @pl.when(usual)
        def _():
            each(lambda i: advance(i, a_prev, b_prev), 1, TX - 1)

        @pl.when(middle)
        def _():
            each(lambda i: turn(i, a_prev, b_prev), 1, TX - 1)

        for c in range(3):
            for i in range(TX):
                cl[c, i : i + 1] = D[c, i * TY : i * TY + 1]
                cr[c, i : i + 1] = D[c, (i + 1) * TY - 1 : (i + 1) * TY]
        to_right = remote(cr, lf.at[par], S_LF, R_LF + par, (px, py_next))
        to_left = remote(cl, rt.at[par], S_RT, R_RT + par, (px, py_prev))
        to_right.start()
        to_left.start()

        @pl.when(middle)
        def _():
            for c in range(3):
                for i in range(TX):
                    c0S[c, i : i + 1] = S[c, i * TY : i * TY + 1]
            save_shape.start()
            shape_down.start()
            shape_right.start()

        wait_bytes(recv1.at[pl.ds(0, half - 1)], R_P1)
        for c in range(3):
            high, low = split2(recv1[:, c].reshape(SLOTS, V))
            matrix = L3[...]
            put(Fs, c, dot(matrix, jnp.concatenate([high, high], 0)) + dot(matrix[:, :SLOTS], low))
        for h, q in peers:
            to = h * half + q
            remote(Fs.at[to], frecv.at[par, py], S_P2, R_P2 + par, (px, to)).start()
        frecv[par, py] = Fs[py]

        @pl.when(t == 0)
        def _():
            wait_bytes(dq_s.at[pl.ds(0, n_py - 1)], S_DQ)
            load_t.wait()
            gather(T, t_l)

        @pl.when(t == ROUNDS + 1)
        def _():
            wait_bytes(recvS.at[pl.ds(0, n_py - 1)], R_SH)
            wait_bytes(recvS.at[pl.ds(0, n_py - 1)], S_SH)
            stretches(recvS, True)

        to_right.wait()
        to_left.wait()
        each(
            lambda i: stencil(
                i, par, lambda c: D[c, spans(i - 1)], lambda c: D[c, spans(i + 1)]
            ),
            1,
            TX - 1,
        )
        to_next.wait()
        to_prev.wait()
        stencil(0, par, lambda c: up[par, c], lambda c: D[c, spans(1)])
        stencil(TX - 1, par, lambda c: D[c, spans(TX - 2)], lambda c: dn[par, c])
        gather(R, rg_l)
        wait_bytes(recv1.at[pl.ds(0, half - 1)], S_P1)

        wait_bytes(frecv.at[0, pl.ds(0, n_py - 1)], R_P2 + par)
        for c in range(3):
            high, low = split2((frecv[par, 0:half, c] + frecv[par, half:, c]).reshape(SLOTS, V))
            lanes = pl.ds(c * V, V)
            F2[0:SLOTS, lanes] = high
            F2[SLOTS:, lanes] = low
        at_node = dot(CR[...], F2[...])
        for c in range(3):
            r = rg_l[c] - at_node[:SLOTS, c * V : (c + 1) * V]
            d = a_next * d_l[c] + (b_next * inv_l[...]) * r
            d_l[c] = d
            x_l[c] = x_l[c] + d
            put(Y, c, d)
        SF[0:TY] = at_node[SLOTS : SLOTS + TY]
        SF[NODES - TY :] = at_node[SLOTS + TY :]

        @pl.when(t == ROUNDS - 1)
        def _():
            for c in range(3):
                put(XS, c, x_l[c])
                d = inv_l[...] * (x_l[c] - t_l[c]) * (1.0 / THETA)
                d_l[c] = d
                x_l[c] = d
                put(Y, c, d)

        @pl.when(t != last - 1)
        def _():
            send_lent()

        @pl.when(t == ROUNDS - 1)
        def _():
            send_all(XS, recvS, S_SH, R_SH)

        wait_bytes(frecv.at[0, pl.ds(0, n_py - 1)], S_P2)
        return carry

    lax.fori_loop(0, last, round_, 0)

    for c in range(3):
        put(Y, c, x_l[c])
    send_all(Y, recvA, S_AD, R_AD)
    a, b = COEF[-1]
    advance(0, a, b)
    adjoint_down = remote(X.at[:, pl.ds(0, TY)], gdA, S_HD, R_HD, (px_prev, py))
    adjoint_down.start()
    scatter(1, TX - 1)
    each(lambda i: advance(i, a, b), 1, TX)
    save_adjoint = pltpu.make_async_copy(X, adjoint_out, sem.at[L_A])
    save_adjoint.start()
    for c in range(3):
        for i in range(TX):
            c0A[c, i : i + 1] = X[c, i * TY : i * TY + 1]
    adjoint_right = remote(c0A, grA, S_HR, R_HR, (px, py_prev))
    adjoint_right.start()


    def lane_sums(values):
        ones = jnp.ones((8, V), BF16)
        out = None
        for part in split3(values):
            piece = dot_t(ones, part)
            out = piece if out is None else out + piece
        return out[0:1] * (-1.0 / V)

    shape_down.wait()
    shape_right.wait()

    def down(i, below_s, below_a):
        at = spans(i)
        total = None
        for c in range(3):
            term = (X[c, at] - below_a(c)) * (S[c, at] - below_s(c))
            total = term if total is None else total + term
        PD[at] = total

    each(
        lambda i: down(i, lambda c: S[c, spans(i + 1)], lambda c: X[c, spans(i + 1)]), 0, TX - 1
    )
    adjoint_right.wait()

    def beside(i):
        at = spans(i)
        row = iota((TY, V), 0)
        total = None
        for c in range(3):
            s, x = S[c, at], X[c, at]
            s_next = jnp.where(row == TY - 1, grS[c, pl.ds(i, 1), :], pltpu.roll(s, TY - 1, 0))
            x_next = jnp.where(row == TY - 1, grA[c, pl.ds(i, 1), :], pltpu.roll(x, TY - 1, 0))
            term = (x - x_next) * (s - s_next)
            total = term if total is None else total + term
        PR[at] = total

    each(beside, 0, TX)
    right_sums = lane_sums(PR[...])
    adjoint_down.wait()
    down(TX - 1, lambda c: gdS[c], lambda c: gdA[c])
    down_sums = lane_sums(PD[...])
    for i in range(TX):
        lanes = slice(i * TY, (i + 1) * TY)
        down_out[i : i + 1] = down_sums[:, lanes]
        right_out[i : i + 1] = right_sums[:, lanes]
    down_out[...] = jnp.where(gi < n_px * TX - 1, down_out[...], 0.0)
    right_out[...] = jnp.where(gj < n_py * TY - 1, right_out[...], 0.0)

    wait_bytes(recvA.at[pl.ds(0, n_py - 1)], R_AD)
    long_sums = lane_sums(stretches(recvA, False))
    long_out[...] = jnp.where(live, long_sums, 0.0)
    wait_bytes(recvA.at[pl.ds(0, n_py - 1)], S_AD)
    save_shape.wait()
    save_adjoint.wait()


def save_kernel(shape_in, adjoint_in, down_in, right_in, long_in, *refs):
    outs, (shape_v, adjoint_v, down_v, right_v, long_v, sem) = refs[:5], refs[5:]
    parts = 4
    rows = NODES // parts
    moves = []
    for src, held, dst in ((shape_in, shape_v, outs[0]), (adjoint_in, adjoint_v, outs[1])):
        for p in range(parts):
            at = (slice(None), pl.ds(p * rows, rows))
            moves.append((src.at[at], held.at[at], dst.at[at]))
    moves += [(down_in, down_v, outs[2]), (right_in, right_v, outs[3]), (long_in, long_v, outs[4])]
    fetch = [pltpu.make_async_copy(a, b, sem.at[0, k]) for k, (a, b, _) in enumerate(moves)]
    store = [pltpu.make_async_copy(b, c, sem.at[1, k]) for k, (_, b, c) in enumerate(moves)]
    for copy in fetch:
        copy.start()
    for k, copy in enumerate(fetch):
        copy.wait()
        store[k].start()
    for copy in store:
        copy.wait()


def per_device(
    n_px, n_py,
    loads, targets, anchor, q_down, q_right, send_rows, cable_a, cable_b, cable_count, cable_q,
):
    half = n_py // 2
    field = (3, NODES, V)
    vmem = pl.BlockSpec(memory_space=pltpu.VMEM)
    smem = pl.BlockSpec(memory_space=pltpu.SMEM)
    anywhere = pl.BlockSpec(memory_space=pl.ANY)

    def scratch(*shape, dtype=F32):
        return pltpu.VMEM(shape, dtype)

    lent = (half, 3, 8, V)
    results = pl.pallas_call(
        functools.partial(kernel, n_px, n_py),
        out_shape=(
            jax.ShapeDtypeStruct(field, F32),
            jax.ShapeDtypeStruct(field, F32),
            jax.ShapeDtypeStruct((TX, TY), F32),
            jax.ShapeDtypeStruct((TX, TY), F32),
            jax.ShapeDtypeStruct((1, 128), F32),
        ),
        in_specs=[anywhere] * 5 + [smem] + [anywhere] * 3 + [smem, anywhere],
        out_specs=(anywhere, anywhere, vmem, vmem, vmem),
        scratch_shapes=[
            scratch(*field),
            scratch(*field),
            scratch(*field),
            scratch(*field),
            scratch(*field),
            scratch(NODES, 3 * V),
            scratch(NODES, V),
            scratch(NODES + TY, V),
            scratch(NODES, V),
            scratch(NODES, V),
            scratch(NODES, V),
            scratch(NODES, 2 * SLOTS, dtype=BF16),
            scratch(2 * SLOTS, 3 * V, dtype=BF16),
            scratch(SLOTS + 2 * TY, 2 * SLOTS, dtype=BF16),
            scratch(128, 2 * SLOTS, dtype=BF16),
            scratch(128, 128),
            scratch(128, 128),
            scratch(3, SLOTS, V),
            scratch(3, SLOTS, V),
            scratch(3, SLOTS, V),
            scratch(3, SLOTS, V),
            scratch(SLOTS, V),
            scratch(*lent),
            scratch(*lent),
            scratch(*lent),
            scratch(n_py, 3, 8, V),
            scratch(n_py, 3, 8, V),
            scratch(n_py, 3, 8, V),
            scratch(2, n_py, 3, 8, V),
            scratch(2, 3, TY, V),
            scratch(2, 3, TY, V),
            scratch(2, 3, TX, V),
            scratch(2, 3, TX, V),
            scratch(3, TX, V),
            scratch(3, TX, V),
            scratch(8, 128),
            scratch(8, 128),
            scratch(n_py, 8, 128),
            scratch(n_py, 8, 128),
            scratch(8, 128),
            scratch(8, 128),
            scratch(TX, 128),
            scratch(TX, 128),
            scratch(3, TY, V),
            scratch(3, TX, V),
            scratch(3, TY, V),
            scratch(3, TX, V),
            scratch(3, TX, V),
            scratch(3, TX, V),
            scratch(3, 128, V),
            scratch(NODES, V),
            scratch(NODES, V),
            scratch(TX, TY),
            scratch(TX, TY),
            scratch(TX, TY),
            scratch(1, SLOTS, dtype=jnp.int32),
            scratch(1, 128, dtype=jnp.int32),
            scratch(1, 128, dtype=jnp.int32),
            scratch(1, 128),
            pltpu.SemaphoreType.DMA((N_SEM,)),
        ],
        compiler_params=pltpu.CompilerParams(
            collective_id=0, has_side_effects=True, vmem_limit_bytes=LIMIT
        ),
        name="cable_net",
    )(
        loads.reshape(field),
        targets.reshape(field),
        anchor,
        q_down,
        q_right,
        send_rows,
        send_rows,
        cable_a,
        cable_b,
        cable_count,
        cable_q,
    )
    shape_field, adjoint_field, grad_down, grad_right, grad_long = pl.pallas_call(
        save_kernel,
        out_shape=[jax.ShapeDtypeStruct(r.shape, F32) for r in results],
        in_specs=[anywhere] * 5,
        out_specs=[anywhere] * 5,
        scratch_shapes=[pltpu.VMEM(r.shape, F32) for r in results]
        + [pltpu.SemaphoreType.DMA((2, 11))],
        compiler_params=pltpu.CompilerParams(vmem_limit_bytes=LIMIT),
        name="save",
    )(*results)
    tile = (3, TX, TY, V)
    return shape_field.reshape(tile), adjoint_field.reshape(tile), grad_down, grad_right, grad_long


def solution(mesh):
    field = P(None, "px", "py", None)
    flat = P("px", "py")
    return jax.shard_map(
        functools.partial(per_device, mesh.shape["px"], mesh.shape["py"]),
        mesh=mesh,
        in_specs=(field, field) + (flat,) * 8,
        out_specs=(field, field, flat, flat, flat),
        check_vma=False,
    )
```

```python
import functools

import jax
import jax.numpy as jnp
from jax import lax
from jax.experimental import pallas as pl
from jax.experimental.pallas import tpu as pltpu
from jax.sharding import PartitionSpec as P

MESH = pl.DeviceIdType.MESH
F32 = jnp.float32
BF16 = jnp.bfloat16
HIGHEST = lax.Precision.HIGHEST

STEPS = 7
ROUNDS = STEPS - 1
TX, TY, V = 16, 64, 128
NODES = TX * TY
SLOTS = 64
LOW, HIGH = 0.05, 2.0
LIMIT = 60 << 20
THETA = (HIGH + LOW) / 2.0
DELTA = (HIGH - LOW) / 2.0


def coefficients():
    sigma = THETA / DELTA
    rho = 1.0 / sigma
    pairs = []
    for _ in range(ROUNDS):
        rho_new = 1.0 / (2.0 * sigma - rho)
        pairs.append((rho_new * rho, 2.0 * rho_new / DELTA))
        rho = rho_new
    return pairs


COEF = coefficients()


def coef_of(round_):
    a, b = (jnp.float32(value) for value in COEF[-1])
    for k in range(ROUNDS - 1):
        a = jnp.where(round_ == k, jnp.float32(COEF[k][0]), a)
        b = jnp.where(round_ == k, jnp.float32(COEF[k][1]), b)
    return a, b


def split2(x):
    high = x.astype(BF16)
    return high, (x - high.astype(F32)).astype(BF16)


def split3(x):
    high = x.astype(BF16)
    rest = x - high.astype(F32)
    mid = rest.astype(BF16)
    return high, mid, (rest - mid.astype(F32)).astype(BF16)


def dot(a, b):
    return jnp.dot(a, b, preferred_element_type=F32)


def dot_t(a, b, precision=None):
    return lax.dot_general(
        a, b, (((1,), (1,)), ((), ())), precision=precision, preferred_element_type=F32
    )


def iota(shape, dim):
    return lax.broadcasted_iota(jnp.int32, shape, dim)


(
    S_P1, R_P1, S_P2, R_P2, S_UP, R_UP, S_DN, R_DN, S_LF, R_LF, S_RT, R_RT,
    ONES,
) = range(0, 78, 6)
(
    S_CAB, R_CAB, S_DQ, R_DQ, S_QD, R_QD, S_QR, R_QR, S_SH, R_SH, S_AD, R_AD,
    S_GD, R_GD, S_GR, R_GR, S_HD, R_HD, S_HR, R_HR, L_B, L_T, L_S, L_A,
    L_0, L_1, L_2, L_3, L_4, L_5, L_6,
) = range(ONES, ONES + 31)
N_SEM = ONES + 31


def kernel(
    n_px, n_py,
    loads, targets, anchor_h, q_down_h, q_right_h, rows_s, rows_h, cab_a_h, cab_b_h, count, cab_q_h,
    shape_out, adjoint_out, down_out, right_out, long_out,
    R, D, X, S, T, SF, GD, WD, WR, WL, INV, ONE, F2, CR, L3, IO, IP,
    rg_l, d_l, x_l, t_l, inv_l, Y, XS, recv1, recvS, recvA, Fs, frecv,
    up, dn, lf, rt, cl, cr, cab_s, cab_r, dq_s, dq_r, qd_s, qd_r, qr_s, qr_r,
    gdS, grS, gdA, grA, c0S, c0A, stS, PD, PR,
    anchor, q_down, q_right, rows_v, cab_a, cab_b, cab_q, sem,
):
    px = lax.axis_index("px")
    py = lax.axis_index("py")
    half = n_py // 2
    h0 = py // half
    q0 = py % half
    px_next, px_prev = (px + 1) % n_px, (px + n_px - 1) % n_px
    py_next, py_prev = (py + 1) % n_py, (py + n_py - 1) % n_py

    def remote(src, dst, s, r, to):
        return pltpu.make_async_remote_copy(
            src, dst, sem.at[s], sem.at[r], device_id=to, device_id_type=MESH
        )

    def wait_bytes(view, s):
        pltpu.make_async_copy(view, view, sem.at[s]).wait()

    load_b = pltpu.make_async_copy(loads, R, sem.at[L_B])
    load_t = pltpu.make_async_copy(targets, T, sem.at[L_T])
    small = [
        pltpu.make_async_copy(src, dst, sem.at[s])
        for src, dst, s in (
            (cab_a_h, cab_a, L_0), (cab_b_h, cab_b, L_1),
            (cab_q_h, cab_q, L_3), (q_down_h, q_down, L_4), (q_right_h, q_right, L_5),
            (rows_h, rows_v, L_2), (anchor_h, anchor, L_6),
        )
    ]
    for copy in small:
        copy.start()
    load_b.start()
    load_t.start()

    barrier = pltpu.get_barrier_semaphore()
    for i in range(1, n_py):
        pl.semaphore_signal(barrier, inc=1, device_id=(px, (py + i) % n_py), device_id_type=MESH)
    pl.semaphore_signal(barrier, inc=1, device_id=(px_next, py), device_id_type=MESH)
    pl.semaphore_signal(barrier, inc=1, device_id=(px_prev, py), device_id_type=MESH)

    wide = half // 2
    y0, c0 = q0 // 2, q0 % 2
    order = sorted(
        (v for v in ((dx, dy, dc) for dx in (0, 1) for dy in range(wide) for dc in (0, 1)) if any(v)),
        key=lambda v: -(2 * v[0] + min(v[1], wide - v[1])),
    )

    def other(dx, dy, dc):
        return (h0 + dx) % 2, (y0 + dy) % wide * 2 + (c0 + dc) % 2

    peers = [other(*v) for v in order]
    near_peers = [other(*v) for v in order if v[0] == 0]

    for copy in small:
        copy.wait()

    live = iota((1, 128), 1) < count[0, 0]
    q_live = jnp.where(live, cab_q[...], 0.0)
    row8 = iota((8, 128), 0)
    cab_s[...] = jnp.where(
        row8 == 0,
        cab_a[...].astype(F32),
        jnp.where(row8 == 1, cab_b[...].astype(F32), jnp.where(row8 == 2, q_live, 0.0)),
    )
    m_id = iota((128, 128), 0)
    code = (m_id // 8 * 4 + m_id % 4).astype(F32)
    m_half = m_id % 8 // 4

    def ends(values, which):
        mine = m_half == which
        at_a = jnp.where(mine & (code == values[0:1]), 1.0, 0.0)
        at_b = jnp.where(mine & (code == values[1:2]), 1.0, 0.0)
        return at_a, at_b

    at_a, at_b = ends(cab_s[...], h0)
    slot_q = jnp.sum((at_a + at_b) * q_live, axis=1, keepdims=True)
    dq_s[...] = jnp.broadcast_to(slot_q, (128, 128)).reshape(n_py, 8, 128)
    qd_s[...] = jnp.concatenate(
        [jnp.broadcast_to(q_down[TX - 1 : TX, :], (8, TY)), jnp.zeros((8, 128 - TY), F32)], axis=1
    )
    qr_s[...] = jnp.concatenate([q_right[...], jnp.zeros((TX, 128 - TY), F32)], axis=1)

    p_id, l_id = iota((SLOTS, 2 * SLOTS), 0), iota((SLOTS, 2 * SLOTS), 1) % SLOTS
    perm = jnp.where(p_id == (l_id // 8 + half * (l_id % 8 // 4)) * 4 + l_id % 4, 1.0, 0.0)
    row_f = jnp.broadcast_to(rows_v[...].astype(F32), (8, SLOTS))
    in_lanes = jnp.dot(row_f, perm, precision=HIGHEST, preferred_element_type=F32)[0:1]
    in_rows = lax.dot_general(
        perm[:, :SLOTS], row_f, (((0,), (1,)), ((), ())), precision=HIGHEST, preferred_element_type=F32
    )[:, 0:1]
    CR[0:SLOTS] = jnp.where(
        jnp.broadcast_to(in_rows, (SLOTS, 2 * SLOTS)) == in_lanes, 1.0, 0.0
    ).astype(BF16)

    def one_hot(i, carry):
        node = (iota((TY, 2 * SLOTS), 0) + i * TY).astype(F32)
        ONE[pl.ds(pl.multiple_of(i * TY, TY), TY)] = jnp.where(node == in_lanes, 1.0, 0.0).astype(BF16)
        return carry

    lax.fori_loop(0, TX, one_hot, 0)
    CR[SLOTS : SLOTS + TY] = ONE[0:TY]
    CR[SLOTS + TY :] = ONE[NODES - TY :]

    pl.semaphore_wait(barrier, n_py + 1)

    for h, q in peers:
        t = h * half + q
        remote(dq_s.at[t], dq_r.at[py], S_DQ, R_DQ, (px, t)).start()
    cab_copy = remote(cab_s, cab_r, S_CAB, R_CAB, (px, (py + half) % n_py))
    qd_copy = remote(qd_s, qd_r, S_QD, R_QD, (px_next, py))
    qr_copy = remote(qr_s, qr_r, S_QR, R_QR, (px, py_next))
    cab_copy.start()
    qd_copy.start()
    qr_copy.start()
    dq_r[py] = dq_s[py]

    qd_copy.wait()
    qr_copy.wait()
    gi = iota((TX, TY), 0) + px * TX
    gj = iota((TX, TY), 1) + py * TY
    w_down = jnp.where(gi < n_px * TX - 1, q_down[...], 0.0)
    w_right = jnp.where(gj < n_py * TY - 1, q_right[...], 0.0)
    prev_down = jnp.where(px > 0, qd_r[0:1, :TY], 0.0)
    prev_right = jnp.where(py > 0, qr_r[:, TY - 1 : TY], 0.0)
    w_up = jnp.concatenate([prev_down, w_down[:-1]], 0)
    w_left = jnp.concatenate([prev_right, w_right[:, :-1]], 1)
    diag = anchor[...] + w_down + w_up + w_right + w_left
    stacked = jnp.concatenate(
        [diag, w_down, w_right, w_left, jnp.broadcast_to(prev_down, (8, TY))], 0
    )
    eye = jnp.where(iota((TY, TY), 0) == iota((TY, TY), 1), 1.0, 0.0)
    columns = dot_t(eye, stacked, HIGHEST)

    def spread(col):
        return jnp.broadcast_to(columns[:, col : col + 1], (TY, V))

    WD[0:TY] = spread(4 * TX)
    for i in range(TX):
        at = pl.ds(i * TY, TY)
        GD[at] = spread(i)
        WD[pl.ds((i + 1) * TY, TY)] = spread(TX + i)
        WR[at] = spread(2 * TX + i)
        WL[at] = spread(3 * TX + i)

    cab_copy.wait()
    pa, pb = ends(cab_r[...], 1 - h0)
    inc_own, inc_other = at_a - at_b, pa - pb
    IO[...] = inc_own
    IP[...] = inc_other
    of_half = pl.ds(pl.multiple_of(h0 * SLOTS, SLOTS), SLOTS)
    matrix = dot_t(inc_own * q_live, IO[of_half], HIGHEST) + dot_t(
        inc_other * cab_r[2:3], IP[of_half], HIGHEST
    )
    L3[...] = jnp.concatenate([matrix, matrix - matrix.astype(BF16).astype(F32)], 1).astype(BF16)

    def gather(src, dst, comps=(0, 1, 2)):
        def rows_of(w, carry):
            for e in range(8):
                node = rows_s[0, (w + half * (e // 4)) * 4 + e % 4]
                for c in comps:
                    dst[c, pl.ds(w * 8 + e, 1), :] = src[c, pl.ds(node, 1), :]
            return carry

        lax.fori_loop(0, half, rows_of, 0)

    def gather_diag(w, carry):
        for e in range(8):
            node = rows_s[0, (w + half * (e // 4)) * 4 + e % 4]
            inv_l[pl.ds(w * 8 + e, 1), :] = GD[pl.ds(node, 1), :]
        return carry

    def send_all(src, dst, s, r):
        for h, q in peers:
            remote(src.at[:, q], dst.at[:, py], s, r, (px, h * half + q)).start()
        for c in range(3):
            dst[c, py] = src[c, q0]

    def send_lent(c):
        for h, q in near_peers:
            remote(Y.at[c, q], recv1.at[c, q0], S_P1 + c, R_P1 + c, (px, h * half + q)).start()
        recv1[c, q0] = Y[c, q0]

    def put(dst, c, value):
        dst[c] = value.reshape(dst.shape[1], 8, V)

    lax.fori_loop(0, half, gather_diag, 0)
    load_b.wait()
    gather(R, rg_l)

    wait_bytes(dq_r.at[pl.ds(0, n_py - 1)], R_DQ)
    slot_sum = (dq_r[0:half] + dq_r[half:]).reshape(SLOTS, V)
    slot_sum = jnp.concatenate(split2(slot_sum), 0)
    inv_l[...] = 1.0 / (inv_l[...] + dot(CR[0:SLOTS], slot_sum))
    for c in range(3):
        first = inv_l[...] * rg_l[c] * (1.0 / THETA)
        d_l[c] = first
        x_l[c] = first
        put(Y, c, first)
        send_lent(c)
    INV[...] = 1.0 / (GD[...] + dot(ONE[...], slot_sum))

    last = 2 * ROUNDS
    save_shape = pltpu.make_async_copy(S, shape_out, sem.at[L_S])
    shape_down = remote(S.at[:, pl.ds(0, TY)], gdS, S_GD, R_GD, (px_prev, py))
    shape_right = remote(c0S, grS, S_GR, R_GR, (px, py_prev))

    def spans(i):
        return pl.ds(pl.multiple_of(i * TY, TY), TY)

    def lanes(c):
        return slice(c * V, (c + 1) * V)

    def scatter(c):
        SF[TY : NODES - TY, lanes(c)] = dot(ONE[TY : NODES - TY], F2[:, lanes(c)])

    def advance(c, i, a, b):
        at = spans(i)
        r = R[c, at] - SF[at, lanes(c)]
        R[c, at] = r
        d = a * D[c, at] + (INV[at] * b) * r
        D[c, at] = d
        X[c, at] = X[c, at] + d

    def begin(c, i):
        at = spans(i)
        d = INV[at] * (1.0 / THETA) * R[c, at]
        D[c, at] = d
        X[c, at] = d

    def turn(c, i, a, b):
        at = spans(i)
        inv = INV[at]
        r = R[c, at] - SF[at, lanes(c)]
        x = X[c, at] + (a * D[c, at] + (inv * b) * r)
        S[c, at] = x
        r = x - T[c, at]
        R[c, at] = r
        d = inv * r * (1.0 / THETA)
        D[c, at] = d
        X[c, at] = d

    def each(fn, lo, hi):
        def body(i, carry):
            fn(i)
            return carry

        lax.fori_loop(lo, hi, body, 0)

    def stencil(c, i, par, above, below):
        at = spans(i)
        row = iota((TY, V), 0)
        d = D[c, at]
        left = jnp.where(row == 0, lf[par, c, pl.ds(i, 1), :], pltpu.roll(d, 1, 0))
        right = jnp.where(row == TY - 1, rt[par, c, pl.ds(i, 1), :], pltpu.roll(d, TY - 1, 0))
        near = WD[at] * above + WD[spans(i + 1)] * below + WL[at] * left + WR[at] * right
        R[c, at] = R[c, at] - (GD[at] * d - near)

    def rims(c, par):
        which = par * 3 + c
        return (
            remote(
                D.at[c, pl.ds((TX - 1) * TY, TY)], up.at[par, c], S_UP + c, R_UP + which, (px_next, py)
            ),
            remote(D.at[c, pl.ds(0, TY)], dn.at[par, c], S_DN + c, R_DN + which, (px_prev, py)),
        )

    def sides(c, par):
        which = par * 3 + c
        return (
            remote(cr.at[c], lf.at[par, c], S_LF + c, R_LF + which, (px, py_next)),
            remote(cl.at[c], rt.at[par, c], S_RT + c, R_RT + which, (px, py_prev)),
        )

    for c in range(3):
        begin(c, 0)
        begin(c, TX - 1)
        for copy in rims(c, 0):
            copy.start()

    def stretches(view, store):
        at_a_, at_b_ = ends(cab_s[...], h0)
        inc_ = (at_a_ - at_b_).astype(BF16)
        total = None
        for c in range(3):
            out = None
            for part in split3(view[c].reshape(128, V)):
                piece = lax.dot_general(
                    inc_, part, (((0,), (0,)), ((), ())), preferred_element_type=F32
                )
                out = piece if out is None else out + piece
            if store:
                stS[c] = out
            else:
                term = out * stS[c]
                total = term if total is None else total + term
        return total

    def round_(t, carry):
        par = t % 2
        first, middle = t == 0, t == ROUNDS
        usual = jnp.logical_and(t != 0, t != ROUNDS)
        final, half_way = t == last - 1, t == ROUNDS - 1
        a_prev, b_prev = coef_of((t + ROUNDS - 1) % ROUNDS)
        a_next, b_next = coef_of(t % ROUNDS)

        for c in range(3):
            @pl.when(first)
            def _():
                each(lambda i: begin(c, i), 1, TX - 1)

            @pl.when(usual)
            def _():
                scatter(c)
                each(lambda i: advance(c, i, a_prev, b_prev), 1, TX - 1)

            @pl.when(middle)
            def _():
                scatter(c)
                each(lambda i: turn(c, i, a_prev, b_prev), 1, TX - 1)

            for i in range(TX):
                cl[c, i : i + 1] = D[c, i * TY : i * TY + 1]
                cr[c, i : i + 1] = D[c, (i + 1) * TY - 1 : (i + 1) * TY]
            for copy in sides(c, par):
                copy.start()

        for c in range(3):
            wait_bytes(recv1.at[c, pl.ds(0, half - 1)], R_P1 + c)
            high, low = split2(recv1[c].reshape(SLOTS, V))
            matrix = L3[...]
            put(Fs, c, dot(matrix, jnp.concatenate([high, high], 0)) + dot(matrix[:, :SLOTS], low))
            for h, q in peers:
                to = h * half + q
                remote(
                    Fs.at[c, to], frecv.at[par, c, py], S_P2 + c, R_P2 + par * 3 + c, (px, to)
                ).start()
            frecv[par, c, py] = Fs[c, py]

        @pl.when(first)
        def _():
            wait_bytes(dq_s.at[pl.ds(0, n_py - 1)], S_DQ)
            load_t.wait()
            gather(T, t_l)

        @pl.when(middle)
        def _():
            for c in range(3):
                for i in range(TX):
                    c0S[c, i : i + 1] = S[c, i * TY : i * TY + 1]
            save_shape.start()
            shape_down.start()
            shape_right.start()

        @pl.when(t == ROUNDS + 1)
        def _():
            wait_bytes(recvS.at[:, pl.ds(0, n_py - 1)], R_SH)
            wait_bytes(recvS.at[:, pl.ds(0, n_py - 1)], S_SH)
            stretches(recvS, True)

        for c in range(3):
            for copy in sides(c, par):
                copy.wait()
            each(
                lambda i: stencil(c, i, par, D[c, spans(i - 1)], D[c, spans(i + 1)]), 1, TX - 1
            )

        for c in range(3):
            for copy in rims(c, par):
                copy.wait()
            stencil(c, 0, par, up[par, c], D[c, spans(1)])
            stencil(c, TX - 1, par, D[c, spans(TX - 2)], dn[par, c])
            gather(R, rg_l, (c,))
            wait_bytes(recv1.at[c, pl.ds(0, half - 1)], S_P1 + c)
            wait_bytes(frecv.at[0, c, pl.ds(0, n_py - 1)], R_P2 + par * 3 + c)
            high, low = split2((frecv[par, c, 0:half] + frecv[par, c, half:]).reshape(SLOTS, V))
            F2[0:SLOTS, lanes(c)] = high
            F2[SLOTS:, lanes(c)] = low
            at_node = dot(CR[...], F2[:, lanes(c)])
            r = rg_l[c] - at_node[:SLOTS]
            d = a_next * d_l[c] + (b_next * inv_l[...]) * r
            x_l[c] = x_l[c] + d
            d_l[c] = d

            @pl.when(half_way)
            def _():
                put(XS, c, x_l[c])
                d_l[c] = inv_l[...] * (x_l[c] - t_l[c]) * (1.0 / THETA)
                x_l[c] = d_l[c]

            @pl.when(jnp.logical_not(final))
            def _():
                put(Y, c, d_l[c])
                send_lent(c)

            SF[0:TY, lanes(c)] = at_node[SLOTS : SLOTS + TY]
            SF[NODES - TY :, lanes(c)] = at_node[SLOTS + TY :]

            @pl.when(half_way)
            def _():
                turn(c, 0, a_next, b_next)
                turn(c, TX - 1, a_next, b_next)

            @pl.when(jnp.logical_not(half_way))
            def _():
                advance(c, 0, a_next, b_next)
                advance(c, TX - 1, a_next, b_next)

            @pl.when(jnp.logical_not(final))
            def _():
                for copy in rims(c, 1 - par):
                    copy.start()

        @pl.when(half_way)
        def _():
            send_all(XS, recvS, S_SH, R_SH)

        for c in range(3):
            wait_bytes(frecv.at[0, c, pl.ds(0, n_py - 1)], S_P2 + c)
        return carry

    lax.fori_loop(0, last, round_, 0)

    adjoint_down = remote(X.at[:, pl.ds(0, TY)], gdA, S_HD, R_HD, (px_prev, py))
    adjoint_down.start()
    for c in range(3):
        put(Y, c, x_l[c])
    send_all(Y, recvA, S_AD, R_AD)
    a, b = COEF[-1]
    for c in range(3):
        scatter(c)
        each(lambda i: advance(c, i, a, b), 1, TX - 1)
    save_adjoint = pltpu.make_async_copy(X, adjoint_out, sem.at[L_A])
    save_adjoint.start()
    for c in range(3):
        for i in range(TX):
            c0A[c, i : i + 1] = X[c, i * TY : i * TY + 1]
    adjoint_right = remote(c0A, grA, S_HR, R_HR, (px, py_prev))
    adjoint_right.start()


    def lane_sums(values):
        ones = jnp.ones((8, V), BF16)
        out = None
        for part in split3(values):
            piece = dot_t(ones, part)
            out = piece if out is None else out + piece
        return out[0:1] * (-1.0 / V)

    shape_down.wait()
    shape_right.wait()

    def down(i, below_s, below_a):
        at = spans(i)
        total = None
        for c in range(3):
            term = (X[c, at] - below_a(c)) * (S[c, at] - below_s(c))
            total = term if total is None else total + term
        PD[at] = total

    each(
        lambda i: down(i, lambda c: S[c, spans(i + 1)], lambda c: X[c, spans(i + 1)]), 0, TX - 1
    )
    adjoint_right.wait()

    def beside(i):
        at = spans(i)
        row = iota((TY, V), 0)
        total = None
        for c in range(3):
            s, x = S[c, at], X[c, at]
            s_next = jnp.where(row == TY - 1, grS[c, pl.ds(i, 1), :], pltpu.roll(s, TY - 1, 0))
            x_next = jnp.where(row == TY - 1, grA[c, pl.ds(i, 1), :], pltpu.roll(x, TY - 1, 0))
            term = (x - x_next) * (s - s_next)
            total = term if total is None else total + term
        PR[at] = total

    each(beside, 0, TX)
    right_sums = lane_sums(PR[...])
    adjoint_down.wait()
    down(TX - 1, lambda c: gdS[c], lambda c: gdA[c])
    down_sums = lane_sums(PD[...])
    for i in range(TX):
        lanes = slice(i * TY, (i + 1) * TY)
        down_out[i : i + 1] = down_sums[:, lanes]
        right_out[i : i + 1] = right_sums[:, lanes]
    down_out[...] = jnp.where(gi < n_px * TX - 1, down_out[...], 0.0)
    right_out[...] = jnp.where(gj < n_py * TY - 1, right_out[...], 0.0)

    wait_bytes(recvA.at[:, pl.ds(0, n_py - 1)], R_AD)
    long_sums = lane_sums(stretches(recvA, False))
    long_out[...] = jnp.where(live, long_sums, 0.0)
    wait_bytes(recvA.at[:, pl.ds(0, n_py - 1)], S_AD)
    save_shape.wait()
    save_adjoint.wait()


def save_kernel(shape_in, adjoint_in, down_in, right_in, long_in, *refs):
    outs, (shape_v, adjoint_v, down_v, right_v, long_v, sem) = refs[:5], refs[5:]
    parts = 4
    rows = NODES // parts
    moves = []
    for src, held, dst in ((shape_in, shape_v, outs[0]), (adjoint_in, adjoint_v, outs[1])):
        for p in range(parts):
            at = (slice(None), pl.ds(p * rows, rows))
            moves.append((src.at[at], held.at[at], dst.at[at]))
    moves += [(down_in, down_v, outs[2]), (right_in, right_v, outs[3]), (long_in, long_v, outs[4])]
    fetch = [pltpu.make_async_copy(a, b, sem.at[0, k]) for k, (a, b, _) in enumerate(moves)]
    store = [pltpu.make_async_copy(b, c, sem.at[1, k]) for k, (_, b, c) in enumerate(moves)]
    for copy in fetch:
        copy.start()
    for k, copy in enumerate(fetch):
        copy.wait()
        store[k].start()
    for copy in store:
        copy.wait()


def per_device(
    n_px, n_py,
    loads, targets, anchor, q_down, q_right, send_rows, cable_a, cable_b, cable_count, cable_q,
):
    half = n_py // 2
    field = (3, NODES, V)
    vmem = pl.BlockSpec(memory_space=pltpu.VMEM)
    smem = pl.BlockSpec(memory_space=pltpu.SMEM)
    anywhere = pl.BlockSpec(memory_space=pl.ANY)

    def scratch(*shape, dtype=F32):
        return pltpu.VMEM(shape, dtype)

    lent = (3, half, 8, V)
    results = pl.pallas_call(
        functools.partial(kernel, n_px, n_py),
        out_shape=(
            jax.ShapeDtypeStruct(field, F32),
            jax.ShapeDtypeStruct(field, F32),
            jax.ShapeDtypeStruct((TX, TY), F32),
            jax.ShapeDtypeStruct((TX, TY), F32),
            jax.ShapeDtypeStruct((1, 128), F32),
        ),
        in_specs=[anywhere] * 5 + [smem] + [anywhere] * 3 + [smem, anywhere],
        out_specs=(anywhere, anywhere, vmem, vmem, vmem),
        scratch_shapes=[
            scratch(*field),
            scratch(*field),
            scratch(*field),
            scratch(*field),
            scratch(*field),
            scratch(NODES, 3 * V),
            scratch(NODES, V),
            scratch(NODES + TY, V),
            scratch(NODES, V),
            scratch(NODES, V),
            scratch(NODES, V),
            scratch(NODES, 2 * SLOTS, dtype=BF16),
            scratch(2 * SLOTS, 3 * V, dtype=BF16),
            scratch(SLOTS + 2 * TY, 2 * SLOTS, dtype=BF16),
            scratch(128, 2 * SLOTS, dtype=BF16),
            scratch(128, 128),
            scratch(128, 128),
            scratch(3, SLOTS, V),
            scratch(3, SLOTS, V),
            scratch(3, SLOTS, V),
            scratch(3, SLOTS, V),
            scratch(SLOTS, V),
            scratch(*lent),
            scratch(*lent),
            scratch(*lent),
            scratch(3, n_py, 8, V),
            scratch(3, n_py, 8, V),
            scratch(3, n_py, 8, V),
            scratch(2, 3, n_py, 8, V),
            scratch(2, 3, TY, V),
            scratch(2, 3, TY, V),
            scratch(2, 3, TX, V),
            scratch(2, 3, TX, V),
            scratch(3, TX, V),
            scratch(3, TX, V),
            scratch(8, 128),
            scratch(8, 128),
            scratch(n_py, 8, 128),
            scratch(n_py, 8, 128),
            scratch(8, 128),
            scratch(8, 128),
            scratch(TX, 128),
            scratch(TX, 128),
            scratch(3, TY, V),
            scratch(3, TX, V),
            scratch(3, TY, V),
            scratch(3, TX, V),
            scratch(3, TX, V),
            scratch(3, TX, V),
            scratch(3, 128, V),
            scratch(NODES, V),
            scratch(NODES, V),
            scratch(TX, TY),
            scratch(TX, TY),
            scratch(TX, TY),
            scratch(1, SLOTS, dtype=jnp.int32),
            scratch(1, 128, dtype=jnp.int32),
            scratch(1, 128, dtype=jnp.int32),
            scratch(1, 128),
            pltpu.SemaphoreType.DMA((N_SEM,)),
        ],
        compiler_params=pltpu.CompilerParams(
            collective_id=0, has_side_effects=True, vmem_limit_bytes=LIMIT
        ),
        name="cable_net",
    )(
        loads.reshape(field),
        targets.reshape(field),
        anchor,
        q_down,
        q_right,
        send_rows,
        send_rows,
        cable_a,
        cable_b,
        cable_count,
        cable_q,
    )
    shape_field, adjoint_field, grad_down, grad_right, grad_long = pl.pallas_call(
        save_kernel,
        out_shape=[jax.ShapeDtypeStruct(r.shape, F32) for r in results],
        in_specs=[anywhere] * 5,
        out_specs=[anywhere] * 5,
        scratch_shapes=[pltpu.VMEM(r.shape, F32) for r in results]
        + [pltpu.SemaphoreType.DMA((2, 11))],
        compiler_params=pltpu.CompilerParams(vmem_limit_bytes=LIMIT),
        name="save",
    )(*results)
    tile = (3, TX, TY, V)
    return shape_field.reshape(tile), adjoint_field.reshape(tile), grad_down, grad_right, grad_long


def solution(mesh):
    field = P(None, "px", "py", None)
    flat = P("px", "py")
    return jax.shard_map(
        functools.partial(per_device, mesh.shape["px"], mesh.shape["py"]),
        mesh=mesh,
        in_specs=(field, field) + (flat,) * 8,
        out_specs=(field, field, flat, flat, flat),
        check_vma=False,
    )
```

```python
import functools

import jax
import jax.numpy as jnp
from jax import lax
from jax.experimental import pallas as pl
from jax.experimental.pallas import tpu as pltpu
from jax.sharding import PartitionSpec as P

MESH = pl.DeviceIdType.MESH
F32 = jnp.float32
BF16 = jnp.bfloat16
HIGHEST = lax.Precision.HIGHEST

STEPS = 7
ROUNDS = STEPS - 1
TX, TY, V = 16, 64, 128
NODES = TX * TY
SLOTS = 64
LOW, HIGH = 0.05, 2.0
LIMIT = 60 << 20
THETA = (HIGH + LOW) / 2.0
DELTA = (HIGH - LOW) / 2.0


def coefficients():
    sigma = THETA / DELTA
    rho = 1.0 / sigma
    pairs = []
    for _ in range(ROUNDS):
        rho_new = 1.0 / (2.0 * sigma - rho)
        pairs.append((rho_new * rho, 2.0 * rho_new / DELTA))
        rho = rho_new
    return pairs


COEF = coefficients()


def coef_of(round_):
    a, b = (jnp.float32(value) for value in COEF[-1])
    for k in range(ROUNDS - 1):
        a = jnp.where(round_ == k, jnp.float32(COEF[k][0]), a)
        b = jnp.where(round_ == k, jnp.float32(COEF[k][1]), b)
    return a, b


def split2(x):
    high = x.astype(BF16)
    return high, (x - high.astype(F32)).astype(BF16)


def split3(x):
    high = x.astype(BF16)
    rest = x - high.astype(F32)
    mid = rest.astype(BF16)
    return high, mid, (rest - mid.astype(F32)).astype(BF16)


def dot(a, b):
    return jnp.dot(a, b, preferred_element_type=F32)


def dot_t(a, b, precision=None):
    return lax.dot_general(
        a, b, (((1,), (1,)), ((), ())), precision=precision, preferred_element_type=F32
    )


def iota(shape, dim):
    return lax.broadcasted_iota(jnp.int32, shape, dim)


(
    S_P1, R_P1, S_P2, R_P2, S_UP, R_UP, S_DN, R_DN, S_LF, R_LF, S_RT, R_RT,
    ONES,
) = range(0, 78, 6)
(
    S_CAB, R_CAB, S_DQ, R_DQ, S_QD, R_QD, S_QR, R_QR, S_SH, R_SH, S_AD, R_AD,
    S_GD, R_GD, S_GR, R_GR, S_HD, R_HD, S_HR, R_HR, L_B, L_T, L_S, L_A,
    L_0, L_1, L_2, L_3, L_4, L_5, L_6,
) = range(ONES, ONES + 31)
N_SEM = ONES + 31


def kernel(
    n_px, n_py,
    loads, targets, anchor_h, q_down_h, q_right_h, rows_s, rows_h, cab_a_h, cab_b_h, count, cab_q_h,
    shape_out, adjoint_out, down_out, right_out, long_out,
    R, D, X, S, T, SF, GD, WD, WR, WL, INV, ONE, F2, CR, L3, IO, IP,
    rg_l, d_l, x_l, t_l, inv_l, Y, XS, recv1, recvS, recvA, Fs, frecv,
    up, dn, lf, rt, cl, cr, cab_s, cab_r, dq_s, dq_r, qd_s, qd_r, qr_s, qr_r,
    gdS, grS, gdA, grA, c0S, c0A, stS, PD, PR,
    anchor, q_down, q_right, rows_v, cab_a, cab_b, cab_q, sem,
):
    px = lax.axis_index("px")
    py = lax.axis_index("py")
    half = n_py // 2
    h0 = py // half
    q0 = py % half
    px_next, px_prev = (px + 1) % n_px, (px + n_px - 1) % n_px
    py_next, py_prev = (py + 1) % n_py, (py + n_py - 1) % n_py

    def remote(src, dst, s, r, to):
        return pltpu.make_async_remote_copy(
            src, dst, sem.at[s], sem.at[r], device_id=to, device_id_type=MESH
        )

    def wait_bytes(view, s):
        pltpu.make_async_copy(view, view, sem.at[s]).wait()

    load_b = pltpu.make_async_copy(loads, R, sem.at[L_B])
    load_t = pltpu.make_async_copy(targets, T, sem.at[L_T])
    small = [
        pltpu.make_async_copy(src, dst, sem.at[s])
        for src, dst, s in (
            (cab_a_h, cab_a, L_0), (cab_b_h, cab_b, L_1),
            (cab_q_h, cab_q, L_3), (q_down_h, q_down, L_4), (q_right_h, q_right, L_5),
            (rows_h, rows_v, L_2), (anchor_h, anchor, L_6),
        )
    ]
    for copy in small:
        copy.start()
    load_b.start()
    load_t.start()

    barrier = pltpu.get_barrier_semaphore()
    for i in range(1, n_py):
        pl.semaphore_signal(barrier, inc=1, device_id=(px, (py + i) % n_py), device_id_type=MESH)
    pl.semaphore_signal(barrier, inc=1, device_id=(px_next, py), device_id_type=MESH)
    pl.semaphore_signal(barrier, inc=1, device_id=(px_prev, py), device_id_type=MESH)

    wide = half // 2
    y0, c0 = q0 // 2, q0 % 2
    order = sorted(
        (v for v in ((dx, dy, dc) for dx in (0, 1) for dy in range(wide) for dc in (0, 1)) if any(v)),
        key=lambda v: -(2 * v[0] + min(v[1], wide - v[1])),
    )

    def other(dx, dy, dc):
        return (h0 + dx) % 2, (y0 + dy) % wide * 2 + (c0 + dc) % 2

    peers = [other(*v) for v in order]
    near_peers = [other(*v) for v in order if v[0] == 0]

    for copy in small:
        copy.wait()

    live = iota((1, 128), 1) < count[0, 0]
    q_live = jnp.where(live, cab_q[...], 0.0)
    row8 = iota((8, 128), 0)
    cab_s[...] = jnp.where(
        row8 == 0,
        cab_a[...].astype(F32),
        jnp.where(row8 == 1, cab_b[...].astype(F32), jnp.where(row8 == 2, q_live, 0.0)),
    )
    m_id = iota((128, 128), 0)
    code = (m_id // 8 * 4 + m_id % 4).astype(F32)
    m_half = m_id % 8 // 4

    def ends(values, which):
        mine = m_half == which
        at_a = jnp.where(mine & (code == values[0:1]), 1.0, 0.0)
        at_b = jnp.where(mine & (code == values[1:2]), 1.0, 0.0)
        return at_a, at_b

    at_a, at_b = ends(cab_s[...], h0)
    slot_q = jnp.sum((at_a + at_b) * q_live, axis=1, keepdims=True)
    dq_s[...] = jnp.broadcast_to(slot_q, (128, 128)).reshape(n_py, 8, 128)
    qd_s[...] = jnp.concatenate(
        [jnp.broadcast_to(q_down[TX - 1 : TX, :], (8, TY)), jnp.zeros((8, 128 - TY), F32)], axis=1
    )
    qr_s[...] = jnp.concatenate([q_right[...], jnp.zeros((TX, 128 - TY), F32)], axis=1)

    p_id, l_id = iota((SLOTS, 2 * SLOTS), 0), iota((SLOTS, 2 * SLOTS), 1) % SLOTS
    perm = jnp.where(p_id == (l_id // 8 + half * (l_id % 8 // 4)) * 4 + l_id % 4, 1.0, 0.0)
    row_f = jnp.broadcast_to(rows_v[...].astype(F32), (8, SLOTS))
    in_lanes = jnp.dot(row_f, perm, precision=HIGHEST, preferred_element_type=F32)[0:1]
    in_rows = lax.dot_general(
        perm[:, :SLOTS], row_f, (((0,), (1,)), ((), ())), precision=HIGHEST, preferred_element_type=F32
    )[:, 0:1]
    CR[0:SLOTS] = jnp.where(
        jnp.broadcast_to(in_rows, (SLOTS, 2 * SLOTS)) == in_lanes, 1.0, 0.0
    ).astype(BF16)

    def one_hot(i, carry):
        node = (iota((TY, 2 * SLOTS), 0) + i * TY).astype(F32)
        ONE[pl.ds(pl.multiple_of(i * TY, TY), TY)] = jnp.where(node == in_lanes, 1.0, 0.0).astype(BF16)
        return carry

    lax.fori_loop(0, TX, one_hot, 0)
    CR[SLOTS : SLOTS + TY] = ONE[0:TY]
    CR[SLOTS + TY :] = ONE[NODES - TY :]

    pl.semaphore_wait(barrier, n_py + 1)

    for h, q in peers:
        t = h * half + q
        remote(dq_s.at[t], dq_r.at[py], S_DQ, R_DQ, (px, t)).start()
    cab_copy = remote(cab_s, cab_r, S_CAB, R_CAB, (px, (py + half) % n_py))
    qd_copy = remote(qd_s, qd_r, S_QD, R_QD, (px_next, py))
    qr_copy = remote(qr_s, qr_r, S_QR, R_QR, (px, py_next))
    cab_copy.start()
    qd_copy.start()
    qr_copy.start()
    dq_r[py] = dq_s[py]

    qd_copy.wait()
    qr_copy.wait()
    gi = iota((TX, TY), 0) + px * TX
    gj = iota((TX, TY), 1) + py * TY
    w_down = jnp.where(gi < n_px * TX - 1, q_down[...], 0.0)
    w_right = jnp.where(gj < n_py * TY - 1, q_right[...], 0.0)
    prev_down = jnp.where(px > 0, qd_r[0:1, :TY], 0.0)
    prev_right = jnp.where(py > 0, qr_r[:, TY - 1 : TY], 0.0)
    w_up = jnp.concatenate([prev_down, w_down[:-1]], 0)
    w_left = jnp.concatenate([prev_right, w_right[:, :-1]], 1)
    diag = anchor[...] + w_down + w_up + w_right + w_left
    stacked = jnp.concatenate(
        [diag, w_down, w_right, w_left, jnp.broadcast_to(prev_down, (8, TY))], 0
    )
    eye = jnp.where(iota((TY, TY), 0) == iota((TY, TY), 1), 1.0, 0.0)
    columns = dot_t(eye, stacked, HIGHEST)

    def spread(col):
        return jnp.broadcast_to(columns[:, col : col + 1], (TY, V))

    WD[0:TY] = spread(4 * TX)
    for i in range(TX):
        at = pl.ds(i * TY, TY)
        GD[at] = spread(i)
        WD[pl.ds((i + 1) * TY, TY)] = spread(TX + i)
        WR[at] = spread(2 * TX + i)
        WL[at] = spread(3 * TX + i)

    cab_copy.wait()
    pa, pb = ends(cab_r[...], 1 - h0)
    inc_own, inc_other = at_a - at_b, pa - pb
    IO[...] = inc_own
    IP[...] = inc_other
    of_half = pl.ds(pl.multiple_of(h0 * SLOTS, SLOTS), SLOTS)
    matrix = dot_t(inc_own * q_live, IO[of_half], HIGHEST) + dot_t(
        inc_other * cab_r[2:3], IP[of_half], HIGHEST
    )
    L3[...] = jnp.concatenate([matrix, matrix - matrix.astype(BF16).astype(F32)], 1).astype(BF16)

    def gather(src, dst, comps=(0, 1, 2)):
        def rows_of(w, carry):
            for e in range(8):
                node = rows_s[0, (w + half * (e // 4)) * 4 + e % 4]
                for c in comps:
                    dst[c, pl.ds(w * 8 + e, 1), :] = src[c, pl.ds(node, 1), :]
            return carry

        lax.fori_loop(0, half, rows_of, 0)

    def gather_diag(w, carry):
        for e in range(8):
            node = rows_s[0, (w + half * (e // 4)) * 4 + e % 4]
            inv_l[pl.ds(w * 8 + e, 1), :] = GD[pl.ds(node, 1), :]
        return carry

    def send_all(src, dst, s, r):
        for h, q in peers:
            remote(src.at[:, q], dst.at[:, py], s, r, (px, h * half + q)).start()
        for c in range(3):
            dst[c, py] = src[c, q0]

    def send_lent(c):
        for h, q in near_peers:
            remote(Y.at[c, q], recv1.at[c, q0], S_P1 + c, R_P1 + c, (px, h * half + q)).start()
        recv1[c, q0] = Y[c, q0]

    def put(dst, c, value):
        dst[c] = value.reshape(dst.shape[1], 8, V)

    lax.fori_loop(0, half, gather_diag, 0)
    load_b.wait()
    gather(R, rg_l)

    wait_bytes(dq_r.at[pl.ds(0, n_py - 1)], R_DQ)
    slot_sum = (dq_r[0:half] + dq_r[half:]).reshape(SLOTS, V)
    slot_sum = jnp.concatenate(split2(slot_sum), 0)
    inv_l[...] = 1.0 / (inv_l[...] + dot(CR[0:SLOTS], slot_sum))
    for c in range(3):
        first = inv_l[...] * rg_l[c] * (1.0 / THETA)
        d_l[c] = first
        x_l[c] = first
        put(Y, c, first)
        send_lent(c)
    INV[...] = 1.0 / (GD[...] + dot(ONE[...], slot_sum))

    last = 2 * ROUNDS
    save_shape = pltpu.make_async_copy(S, shape_out, sem.at[L_S])
    shape_down = remote(S.at[:, pl.ds(0, TY)], gdS, S_GD, R_GD, (px_prev, py))
    shape_right = remote(c0S, grS, S_GR, R_GR, (px, py_prev))

    def spans(i):
        return pl.ds(pl.multiple_of(i * TY, TY), TY)

    def lanes(c):
        return slice(c * V, (c + 1) * V)

    def scatter(c):
        SF[TY : NODES - TY, lanes(c)] = dot(ONE[TY : NODES - TY], F2[:, lanes(c)])

    def advance(c, i, a, b):
        at = spans(i)
        r = R[c, at] - SF[at, lanes(c)]
        R[c, at] = r
        d = a * D[c, at] + (INV[at] * b) * r
        D[c, at] = d
        X[c, at] = X[c, at] + d

    def begin(c, i):
        at = spans(i)
        d = INV[at] * (1.0 / THETA) * R[c, at]
        D[c, at] = d
        X[c, at] = d

    def turn(c, i, a, b):
        at = spans(i)
        inv = INV[at]
        r = R[c, at] - SF[at, lanes(c)]
        x = X[c, at] + (a * D[c, at] + (inv * b) * r)
        S[c, at] = x
        r = x - T[c, at]
        R[c, at] = r
        d = inv * r * (1.0 / THETA)
        D[c, at] = d
        X[c, at] = d

    def each(fn, lo, hi):
        def body(i, carry):
            fn(i)
            return carry

        lax.fori_loop(lo, hi, body, 0)

    def stencil(c, i, par, above, below):
        at = spans(i)
        row = iota((TY, V), 0)
        d = D[c, at]
        left = jnp.where(row == 0, lf[par, c, pl.ds(i, 1), :], pltpu.roll(d, 1, 0))
        right = jnp.where(row == TY - 1, rt[par, c, pl.ds(i, 1), :], pltpu.roll(d, TY - 1, 0))
        near = WD[at] * above + WD[spans(i + 1)] * below + WL[at] * left + WR[at] * right
        R[c, at] = R[c, at] - (GD[at] * d - near)

    def rims(c, par):
        which = par * 3 + c
        return (
            remote(
                D.at[c, pl.ds((TX - 1) * TY, TY)], up.at[par, c], S_UP + c, R_UP + which, (px_next, py)
            ),
            remote(D.at[c, pl.ds(0, TY)], dn.at[par, c], S_DN + c, R_DN + which, (px_prev, py)),
        )

    def early(c):
        return (2, 1, 1)[c]

    def sides(c, par):
        which = par * 3 + c
        return (
            remote(cr.at[c], lf.at[par, c], S_LF + c, R_LF + which, (px, py_next)),
            remote(cl.at[c], rt.at[par, c], S_RT + c, R_RT + which, (px, py_prev)),
        )

    for c in range(3):
        begin(c, 0)
        begin(c, TX - 1)
        for copy in rims(c, 0)[: early(c)]:
            copy.start()

    def stretches(view, store):
        at_a_, at_b_ = ends(cab_s[...], h0)
        inc_ = (at_a_ - at_b_).astype(BF16)
        total = None
        for c in range(3):
            out = None
            for part in split3(view[c].reshape(128, V)):
                piece = lax.dot_general(
                    inc_, part, (((0,), (0,)), ((), ())), preferred_element_type=F32
                )
                out = piece if out is None else out + piece
            if store:
                stS[c] = out
            else:
                term = out * stS[c]
                total = term if total is None else total + term
        return total

    def round_(t, carry):
        par = t % 2
        first, middle = t == 0, t == ROUNDS
        usual = jnp.logical_and(t != 0, t != ROUNDS)
        final, half_way = t == last - 1, t == ROUNDS - 1
        a_prev, b_prev = coef_of((t + ROUNDS - 1) % ROUNDS)
        a_next, b_next = coef_of(t % ROUNDS)

        for c in range(3):
            @pl.when(first)
            def _():
                each(lambda i: begin(c, i), 1, TX - 1)

            @pl.when(usual)
            def _():
                scatter(c)
                each(lambda i: advance(c, i, a_prev, b_prev), 1, TX - 1)

            @pl.when(middle)
            def _():
                scatter(c)
                each(lambda i: turn(c, i, a_prev, b_prev), 1, TX - 1)

            for i in range(TX):
                cl[c, i : i + 1] = D[c, i * TY : i * TY + 1]
                cr[c, i : i + 1] = D[c, (i + 1) * TY - 1 : (i + 1) * TY]
            for copy in sides(c, par):
                copy.start()

        for c in range(3):
            wait_bytes(recv1.at[c, pl.ds(0, half - 1)], R_P1 + c)
            high, low = split2(recv1[c].reshape(SLOTS, V))
            matrix = L3[...]
            put(Fs, c, dot(matrix, jnp.concatenate([high, high], 0)) + dot(matrix[:, :SLOTS], low))
            for h, q in peers:
                to = h * half + q
                remote(
                    Fs.at[c, to], frecv.at[par, c, py], S_P2 + c, R_P2 + par * 3 + c, (px, to)
                ).start()
            frecv[par, c, py] = Fs[c, py]
            for copy in rims(c, par)[early(c) :]:
                copy.start()

        @pl.when(first)
        def _():
            wait_bytes(dq_s.at[pl.ds(0, n_py - 1)], S_DQ)
            load_t.wait()
            gather(T, t_l)

        @pl.when(middle)
        def _():
            for c in range(3):
                for i in range(TX):
                    c0S[c, i : i + 1] = S[c, i * TY : i * TY + 1]
            save_shape.start()
            shape_down.start()
            shape_right.start()

        @pl.when(t == ROUNDS + 1)
        def _():
            wait_bytes(recvS.at[:, pl.ds(0, n_py - 1)], R_SH)
            wait_bytes(recvS.at[:, pl.ds(0, n_py - 1)], S_SH)
            stretches(recvS, True)

        for c in range(3):
            for copy in sides(c, par):
                copy.wait()
            each(
                lambda i: stencil(c, i, par, D[c, spans(i - 1)], D[c, spans(i + 1)]), 1, TX - 1
            )

        for c in range(3):
            for copy in rims(c, par):
                copy.wait()
            stencil(c, 0, par, up[par, c], D[c, spans(1)])
            stencil(c, TX - 1, par, D[c, spans(TX - 2)], dn[par, c])
            gather(R, rg_l, (c,))
            wait_bytes(recv1.at[c, pl.ds(0, half - 1)], S_P1 + c)
            wait_bytes(frecv.at[0, c, pl.ds(0, n_py - 1)], R_P2 + par * 3 + c)
            high, low = split2((frecv[par, c, 0:half] + frecv[par, c, half:]).reshape(SLOTS, V))
            F2[0:SLOTS, lanes(c)] = high
            F2[SLOTS:, lanes(c)] = low
            at_node = dot(CR[...], F2[:, lanes(c)])
            r = rg_l[c] - at_node[:SLOTS]
            d = a_next * d_l[c] + (b_next * inv_l[...]) * r
            x_l[c] = x_l[c] + d
            d_l[c] = d

            @pl.when(half_way)
            def _():
                put(XS, c, x_l[c])
                d_l[c] = inv_l[...] * (x_l[c] - t_l[c]) * (1.0 / THETA)
                x_l[c] = d_l[c]

            @pl.when(jnp.logical_not(final))
            def _():
                put(Y, c, d_l[c])
                send_lent(c)

            SF[0:TY, lanes(c)] = at_node[SLOTS : SLOTS + TY]
            SF[NODES - TY :, lanes(c)] = at_node[SLOTS + TY :]

            @pl.when(half_way)
            def _():
                turn(c, 0, a_next, b_next)
                turn(c, TX - 1, a_next, b_next)

            @pl.when(jnp.logical_not(half_way))
            def _():
                advance(c, 0, a_next, b_next)
                advance(c, TX - 1, a_next, b_next)

            @pl.when(jnp.logical_not(final))
            def _():
                for copy in rims(c, 1 - par)[: early(c)]:
                    copy.start()

        @pl.when(half_way)
        def _():
            send_all(XS, recvS, S_SH, R_SH)

        for c in range(3):
            wait_bytes(frecv.at[0, c, pl.ds(0, n_py - 1)], S_P2 + c)
        return carry

    lax.fori_loop(0, last, round_, 0)

    adjoint_down = remote(X.at[:, pl.ds(0, TY)], gdA, S_HD, R_HD, (px_prev, py))
    adjoint_down.start()
    for c in range(3):
        put(Y, c, x_l[c])
    send_all(Y, recvA, S_AD, R_AD)
    a, b = COEF[-1]
    for c in range(3):
        scatter(c)
        each(lambda i: advance(c, i, a, b), 1, TX - 1)
    save_adjoint = pltpu.make_async_copy(X, adjoint_out, sem.at[L_A])
    save_adjoint.start()
    for c in range(3):
        for i in range(TX):
            c0A[c, i : i + 1] = X[c, i * TY : i * TY + 1]
    adjoint_right = remote(c0A, grA, S_HR, R_HR, (px, py_prev))
    adjoint_right.start()


    def lane_sums(values):
        ones = jnp.ones((8, V), BF16)
        out = None
        for part in split3(values):
            piece = dot_t(ones, part)
            out = piece if out is None else out + piece
        return out[0:1] * (-1.0 / V)

    shape_down.wait()
    shape_right.wait()

    def down(i, below_s, below_a):
        at = spans(i)
        total = None
        for c in range(3):
            term = (X[c, at] - below_a(c)) * (S[c, at] - below_s(c))
            total = term if total is None else total + term
        PD[at] = total

    each(
        lambda i: down(i, lambda c: S[c, spans(i + 1)], lambda c: X[c, spans(i + 1)]), 0, TX - 1
    )
    adjoint_right.wait()

    def beside(i):
        at = spans(i)
        row = iota((TY, V), 0)
        total = None
        for c in range(3):
            s, x = S[c, at], X[c, at]
            s_next = jnp.where(row == TY - 1, grS[c, pl.ds(i, 1), :], pltpu.roll(s, TY - 1, 0))
            x_next = jnp.where(row == TY - 1, grA[c, pl.ds(i, 1), :], pltpu.roll(x, TY - 1, 0))
            term = (x - x_next) * (s - s_next)
            total = term if total is None else total + term
        PR[at] = total

    each(beside, 0, TX)
    right_sums = lane_sums(PR[...])
    adjoint_down.wait()
    down(TX - 1, lambda c: gdS[c], lambda c: gdA[c])
    down_sums = lane_sums(PD[...])
    for i in range(TX):
        lanes = slice(i * TY, (i + 1) * TY)
        down_out[i : i + 1] = down_sums[:, lanes]
        right_out[i : i + 1] = right_sums[:, lanes]
    down_out[...] = jnp.where(gi < n_px * TX - 1, down_out[...], 0.0)
    right_out[...] = jnp.where(gj < n_py * TY - 1, right_out[...], 0.0)

    wait_bytes(recvA.at[:, pl.ds(0, n_py - 1)], R_AD)
    long_sums = lane_sums(stretches(recvA, False))
    long_out[...] = jnp.where(live, long_sums, 0.0)
    wait_bytes(recvA.at[:, pl.ds(0, n_py - 1)], S_AD)
    save_shape.wait()
    save_adjoint.wait()


def save_kernel(shape_in, adjoint_in, down_in, right_in, long_in, *refs):
    outs, (shape_v, adjoint_v, down_v, right_v, long_v, sem) = refs[:5], refs[5:]
    parts = 4
    rows = NODES // parts
    moves = []
    for src, held, dst in ((shape_in, shape_v, outs[0]), (adjoint_in, adjoint_v, outs[1])):
        for p in range(parts):
            at = (slice(None), pl.ds(p * rows, rows))
            moves.append((src.at[at], held.at[at], dst.at[at]))
    moves += [(down_in, down_v, outs[2]), (right_in, right_v, outs[3]), (long_in, long_v, outs[4])]
    fetch = [pltpu.make_async_copy(a, b, sem.at[0, k]) for k, (a, b, _) in enumerate(moves)]
    store = [pltpu.make_async_copy(b, c, sem.at[1, k]) for k, (_, b, c) in enumerate(moves)]
    for copy in fetch:
        copy.start()
    for k, copy in enumerate(fetch):
        copy.wait()
        store[k].start()
    for copy in store:
        copy.wait()


def per_device(
    n_px, n_py,
    loads, targets, anchor, q_down, q_right, send_rows, cable_a, cable_b, cable_count, cable_q,
):
    half = n_py // 2
    field = (3, NODES, V)
    vmem = pl.BlockSpec(memory_space=pltpu.VMEM)
    smem = pl.BlockSpec(memory_space=pltpu.SMEM)
    anywhere = pl.BlockSpec(memory_space=pl.ANY)

    def scratch(*shape, dtype=F32):
        return pltpu.VMEM(shape, dtype)

    lent = (3, half, 8, V)
    results = pl.pallas_call(
        functools.partial(kernel, n_px, n_py),
        out_shape=(
            jax.ShapeDtypeStruct(field, F32),
            jax.ShapeDtypeStruct(field, F32),
            jax.ShapeDtypeStruct((TX, TY), F32),
            jax.ShapeDtypeStruct((TX, TY), F32),
            jax.ShapeDtypeStruct((1, 128), F32),
        ),
        in_specs=[anywhere] * 5 + [smem] + [anywhere] * 3 + [smem, anywhere],
        out_specs=(anywhere, anywhere, vmem, vmem, vmem),
        scratch_shapes=[
            scratch(*field),
            scratch(*field),
            scratch(*field),
            scratch(*field),
            scratch(*field),
            scratch(NODES, 3 * V),
            scratch(NODES, V),
            scratch(NODES + TY, V),
            scratch(NODES, V),
            scratch(NODES, V),
            scratch(NODES, V),
            scratch(NODES, 2 * SLOTS, dtype=BF16),
            scratch(2 * SLOTS, 3 * V, dtype=BF16),
            scratch(SLOTS + 2 * TY, 2 * SLOTS, dtype=BF16),
            scratch(128, 2 * SLOTS, dtype=BF16),
            scratch(128, 128),
            scratch(128, 128),
            scratch(3, SLOTS, V),
            scratch(3, SLOTS, V),
            scratch(3, SLOTS, V),
            scratch(3, SLOTS, V),
            scratch(SLOTS, V),
            scratch(*lent),
            scratch(*lent),
            scratch(*lent),
            scratch(3, n_py, 8, V),
            scratch(3, n_py, 8, V),
            scratch(3, n_py, 8, V),
            scratch(2, 3, n_py, 8, V),
            scratch(2, 3, TY, V),
            scratch(2, 3, TY, V),
            scratch(2, 3, TX, V),
            scratch(2, 3, TX, V),
            scratch(3, TX, V),
            scratch(3, TX, V),
            scratch(8, 128),
            scratch(8, 128),
            scratch(n_py, 8, 128),
            scratch(n_py, 8, 128),
            scratch(8, 128),
            scratch(8, 128),
            scratch(TX, 128),
            scratch(TX, 128),
            scratch(3, TY, V),
            scratch(3, TX, V),
            scratch(3, TY, V),
            scratch(3, TX, V),
            scratch(3, TX, V),
            scratch(3, TX, V),
            scratch(3, 128, V),
            scratch(NODES, V),
            scratch(NODES, V),
            scratch(TX, TY),
            scratch(TX, TY),
            scratch(TX, TY),
            scratch(1, SLOTS, dtype=jnp.int32),
            scratch(1, 128, dtype=jnp.int32),
            scratch(1, 128, dtype=jnp.int32),
            scratch(1, 128),
            pltpu.SemaphoreType.DMA((N_SEM,)),
        ],
        compiler_params=pltpu.CompilerParams(
            collective_id=0, has_side_effects=True, vmem_limit_bytes=LIMIT
        ),
        name="cable_net",
    )(
        loads.reshape(field),
        targets.reshape(field),
        anchor,
        q_down,
        q_right,
        send_rows,
        send_rows,
        cable_a,
        cable_b,
        cable_count,
        cable_q,
    )
    shape_field, adjoint_field, grad_down, grad_right, grad_long = pl.pallas_call(
        save_kernel,
        out_shape=[jax.ShapeDtypeStruct(r.shape, F32) for r in results],
        in_specs=[anywhere] * 5,
        out_specs=[anywhere] * 5,
        scratch_shapes=[pltpu.VMEM(r.shape, F32) for r in results]
        + [pltpu.SemaphoreType.DMA((2, 11))],
        compiler_params=pltpu.CompilerParams(vmem_limit_bytes=LIMIT),
        name="save",
    )(*results)
    tile = (3, TX, TY, V)
    return shape_field.reshape(tile), adjoint_field.reshape(tile), grad_down, grad_right, grad_long


def solution(mesh):
    field = P(None, "px", "py", None)
    flat = P("px", "py")
    return jax.shard_map(
        functools.partial(per_device, mesh.shape["px"], mesh.shape["py"]),
        mesh=mesh,
        in_specs=(field, field) + (flat,) * 8,
        out_specs=(field, field, flat, flat, flat),
        check_vma=False,
    )
```

```python
import functools

import jax
import jax.numpy as jnp
from jax import lax
from jax.experimental import pallas as pl
from jax.experimental.pallas import tpu as pltpu
from jax.sharding import PartitionSpec as P

MESH = pl.DeviceIdType.MESH
F32 = jnp.float32
BF16 = jnp.bfloat16
HIGHEST = lax.Precision.HIGHEST

STEPS = 7
ROUNDS = STEPS - 1
TX, TY, V = 16, 64, 128
NODES = TX * TY
SLOTS = 64
LOW, HIGH = 0.05, 2.0
LIMIT = 60 << 20
THETA = (HIGH + LOW) / 2.0
DELTA = (HIGH - LOW) / 2.0


def coefficients():
    sigma = THETA / DELTA
    rho = 1.0 / sigma
    pairs = []
    for _ in range(ROUNDS):
        rho_new = 1.0 / (2.0 * sigma - rho)
        pairs.append((rho_new * rho, 2.0 * rho_new / DELTA))
        rho = rho_new
    return pairs


COEF = coefficients()


def coef_of(round_):
    a, b = (jnp.float32(value) for value in COEF[-1])
    for k in range(ROUNDS - 1):
        a = jnp.where(round_ == k, jnp.float32(COEF[k][0]), a)
        b = jnp.where(round_ == k, jnp.float32(COEF[k][1]), b)
    return a, b


def split2(x):
    high = x.astype(BF16)
    return high, (x - high.astype(F32)).astype(BF16)


def split3(x):
    high = x.astype(BF16)
    rest = x - high.astype(F32)
    mid = rest.astype(BF16)
    return high, mid, (rest - mid.astype(F32)).astype(BF16)


def dot(a, b):
    return jnp.dot(a, b, preferred_element_type=F32)


def dot_t(a, b, precision=None):
    return lax.dot_general(
        a, b, (((1,), (1,)), ((), ())), precision=precision, preferred_element_type=F32
    )


def iota(shape, dim):
    return lax.broadcasted_iota(jnp.int32, shape, dim)


(
    S_P1, R_P1, S_P2, R_P2, S_UP, R_UP, S_DN, R_DN, S_LF, R_LF, S_RT, R_RT,
    ONES,
) = range(0, 78, 6)
(
    S_CAB, R_CAB, S_DQ, R_DQ, S_QD, R_QD, S_QR, R_QR, S_SH, R_SH, S_AD, R_AD,
    S_GD, R_GD, S_GR, R_GR, S_HD, R_HD, S_HR, R_HR, L_B, L_T, L_S, L_A,
    L_0, L_1, L_2, L_3, L_4, L_5, L_6,
) = range(ONES, ONES + 31)
N_SEM = ONES + 31


def kernel(
    n_px, n_py,
    loads, targets, anchor_h, q_down_h, q_right_h, rows_s, rows_h, cab_a_h, cab_b_h, count, cab_q_h,
    shape_out, adjoint_out, down_out, right_out, long_out,
    R, D, X, S, T, SF, GD, WD, WR, WL, INV, ONE, F2, CR, L3, IO, IP,
    rg_l, d_l, x_l, t_l, inv_l, Y, XS, recv1, recvS, recvA, Fs, frecv,
    up, dn, lf, rt, cl, cr, cab_s, cab_r, dq_s, dq_r, qd_s, qd_r, qr_s, qr_r,
    gdS, grS, gdA, grA, c0S, c0A, stS, PD, PR,
    anchor, q_down, q_right, rows_v, cab_a, cab_b, cab_q, sem,
):
    px = lax.axis_index("px")
    py = lax.axis_index("py")
    half = n_py // 2
    h0 = py // half
    q0 = py % half
    px_next, px_prev = (px + 1) % n_px, (px + n_px - 1) % n_px
    py_next, py_prev = (py + 1) % n_py, (py + n_py - 1) % n_py

    def remote(src, dst, s, r, to):
        return pltpu.make_async_remote_copy(
            src, dst, sem.at[s], sem.at[r], device_id=to, device_id_type=MESH
        )

    def wait_bytes(view, s):
        pltpu.make_async_copy(view, view, sem.at[s]).wait()

    load_b = pltpu.make_async_copy(loads, R, sem.at[L_B])
    load_t = pltpu.make_async_copy(targets, T, sem.at[L_T])
    small = [
        pltpu.make_async_copy(src, dst, sem.at[s])
        for src, dst, s in (
            (cab_a_h, cab_a, L_0), (cab_b_h, cab_b, L_1),
            (cab_q_h, cab_q, L_3), (q_down_h, q_down, L_4), (q_right_h, q_right, L_5),
            (rows_h, rows_v, L_2), (anchor_h, anchor, L_6),
        )
    ]
    for copy in small:
        copy.start()
    load_b.start()
    load_t.start()

    barrier = pltpu.get_barrier_semaphore()
    for i in range(1, n_py):
        pl.semaphore_signal(barrier, inc=1, device_id=(px, (py + i) % n_py), device_id_type=MESH)
    pl.semaphore_signal(barrier, inc=1, device_id=(px_next, py), device_id_type=MESH)
    pl.semaphore_signal(barrier, inc=1, device_id=(px_prev, py), device_id_type=MESH)

    wide = half // 2
    y0, c0 = q0 // 2, q0 % 2
    order = sorted(
        (v for v in ((dx, dy, dc) for dx in (0, 1) for dy in range(wide) for dc in (0, 1)) if any(v)),
        key=lambda v: -(2 * v[0] + min(v[1], wide - v[1])),
    )

    def other(dx, dy, dc):
        return (h0 + dx) % 2, (y0 + dy) % wide * 2 + (c0 + dc) % 2

    peers = [other(*v) for v in order]
    near_peers = [other(*v) for v in order if v[0] == 0]

    for copy in small:
        copy.wait()

    live = iota((1, 128), 1) < count[0, 0]
    q_live = jnp.where(live, cab_q[...], 0.0)
    row8 = iota((8, 128), 0)
    cab_s[...] = jnp.where(
        row8 == 0,
        cab_a[...].astype(F32),
        jnp.where(row8 == 1, cab_b[...].astype(F32), jnp.where(row8 == 2, q_live, 0.0)),
    )
    m_id = iota((128, 128), 0)
    code = (m_id // 8 * 4 + m_id % 4).astype(F32)
    m_half = m_id % 8 // 4

    def ends(values, which):
        mine = m_half == which
        at_a = jnp.where(mine & (code == values[0:1]), 1.0, 0.0)
        at_b = jnp.where(mine & (code == values[1:2]), 1.0, 0.0)
        return at_a, at_b

    at_a, at_b = ends(cab_s[...], h0)
    slot_q = jnp.sum((at_a + at_b) * q_live, axis=1, keepdims=True)
    dq_s[...] = jnp.broadcast_to(slot_q, (128, 128)).reshape(n_py, 8, 128)
    qd_s[...] = jnp.concatenate(
        [jnp.broadcast_to(q_down[TX - 1 : TX, :], (8, TY)), jnp.zeros((8, 128 - TY), F32)], axis=1
    )
    qr_s[...] = jnp.concatenate([q_right[...], jnp.zeros((TX, 128 - TY), F32)], axis=1)

    p_id, l_id = iota((SLOTS, 2 * SLOTS), 0), iota((SLOTS, 2 * SLOTS), 1) % SLOTS
    perm = jnp.where(p_id == (l_id // 8 + half * (l_id % 8 // 4)) * 4 + l_id % 4, 1.0, 0.0)
    row_f = jnp.broadcast_to(rows_v[...].astype(F32), (8, SLOTS))
    in_lanes = jnp.dot(row_f, perm, precision=HIGHEST, preferred_element_type=F32)[0:1]
    in_rows = lax.dot_general(
        perm[:, :SLOTS], row_f, (((0,), (1,)), ((), ())), precision=HIGHEST, preferred_element_type=F32
    )[:, 0:1]
    CR[0:SLOTS] = jnp.where(
        jnp.broadcast_to(in_rows, (SLOTS, 2 * SLOTS)) == in_lanes, 1.0, 0.0
    ).astype(BF16)

    def one_hot(i, carry):
        node = (iota((TY, 2 * SLOTS), 0) + i * TY).astype(F32)
        ONE[pl.ds(pl.multiple_of(i * TY, TY), TY)] = jnp.where(node == in_lanes, 1.0, 0.0).astype(BF16)
        return carry

    lax.fori_loop(0, TX, one_hot, 0)
    CR[SLOTS : SLOTS + TY] = ONE[0:TY]
    CR[SLOTS + TY :] = ONE[NODES - TY :]

    pl.semaphore_wait(barrier, n_py + 1)

    for h, q in peers:
        t = h * half + q
        remote(dq_s.at[t], dq_r.at[py], S_DQ, R_DQ, (px, t)).start()
    cab_copy = remote(cab_s, cab_r, S_CAB, R_CAB, (px, (py + half) % n_py))
    qd_copy = remote(qd_s, qd_r, S_QD, R_QD, (px_next, py))
    qr_copy = remote(qr_s, qr_r, S_QR, R_QR, (px, py_next))
    cab_copy.start()
    qd_copy.start()
    qr_copy.start()
    dq_r[py] = dq_s[py]

    qd_copy.wait()
    qr_copy.wait()
    gi = iota((TX, TY), 0) + px * TX
    gj = iota((TX, TY), 1) + py * TY
    w_down = jnp.where(gi < n_px * TX - 1, q_down[...], 0.0)
    w_right = jnp.where(gj < n_py * TY - 1, q_right[...], 0.0)
    prev_down = jnp.where(px > 0, qd_r[0:1, :TY], 0.0)
    prev_right = jnp.where(py > 0, qr_r[:, TY - 1 : TY], 0.0)
    w_up = jnp.concatenate([prev_down, w_down[:-1]], 0)
    w_left = jnp.concatenate([prev_right, w_right[:, :-1]], 1)
    diag = anchor[...] + w_down + w_up + w_right + w_left
    stacked = jnp.concatenate(
        [diag, w_down, w_right, w_left, jnp.broadcast_to(prev_down, (8, TY))], 0
    )
    eye = jnp.where(iota((TY, TY), 0) == iota((TY, TY), 1), 1.0, 0.0)
    columns = dot_t(eye, stacked, HIGHEST)

    def spread(col):
        return jnp.broadcast_to(columns[:, col : col + 1], (TY, V))

    WD[0:TY] = spread(4 * TX)
    for i in range(TX):
        at = pl.ds(i * TY, TY)
        GD[at] = spread(i)
        WD[pl.ds((i + 1) * TY, TY)] = spread(TX + i)
        WR[at] = spread(2 * TX + i)
        WL[at] = spread(3 * TX + i)

    cab_copy.wait()
    pa, pb = ends(cab_r[...], 1 - h0)
    inc_own, inc_other = at_a - at_b, pa - pb
    IO[...] = inc_own
    IP[...] = inc_other
    of_half = pl.ds(pl.multiple_of(h0 * SLOTS, SLOTS), SLOTS)
    matrix = dot_t(inc_own * q_live, IO[of_half], HIGHEST) + dot_t(
        inc_other * cab_r[2:3], IP[of_half], HIGHEST
    )
    L3[...] = jnp.concatenate([matrix, matrix - matrix.astype(BF16).astype(F32)], 1).astype(BF16)

    def gather(src, dst, comps=(0, 1, 2)):
        def rows_of(w, carry):
            for e in range(8):
                node = rows_s[0, (w + half * (e // 4)) * 4 + e % 4]
                for c in comps:
                    dst[c, pl.ds(w * 8 + e, 1), :] = src[c, pl.ds(node, 1), :]
            return carry

        lax.fori_loop(0, half, rows_of, 0)

    def gather_diag(w, carry):
        for e in range(8):
            node = rows_s[0, (w + half * (e // 4)) * 4 + e % 4]
            inv_l[pl.ds(w * 8 + e, 1), :] = GD[pl.ds(node, 1), :]
        return carry

    def send_all(src, dst, s, r):
        for h, q in peers:
            remote(src.at[:, q], dst.at[:, py], s, r, (px, h * half + q)).start()
        for c in range(3):
            dst[c, py] = src[c, q0]

    def send_comp(src, dst, c, s, r):
        for h, q in peers:
            remote(src.at[c, q], dst.at[c, py], s, r, (px, h * half + q)).start()
        dst[c, py] = src[c, q0]

    def send_lent(c):
        for h, q in near_peers:
            remote(Y.at[c, q], recv1.at[c, q0], S_P1 + c, R_P1 + c, (px, h * half + q)).start()
        recv1[c, q0] = Y[c, q0]

    def put(dst, c, value):
        dst[c] = value.reshape(dst.shape[1], 8, V)

    lax.fori_loop(0, half, gather_diag, 0)
    load_b.wait()
    gather(R, rg_l)

    wait_bytes(dq_r.at[pl.ds(0, n_py - 1)], R_DQ)
    slot_sum = (dq_r[0:half] + dq_r[half:]).reshape(SLOTS, V)
    slot_sum = jnp.concatenate(split2(slot_sum), 0)
    inv_l[...] = 1.0 / (inv_l[...] + dot(CR[0:SLOTS], slot_sum))
    for c in range(3):
        first = inv_l[...] * rg_l[c] * (1.0 / THETA)
        d_l[c] = first
        x_l[c] = first
        put(Y, c, first)
        send_lent(c)
    on_rims = dot(CR[SLOTS:], slot_sum)
    INV[0:TY] = 1.0 / (GD[0:TY] + on_rims[:TY])
    INV[NODES - TY :] = 1.0 / (GD[NODES - TY :] + on_rims[TY:])

    last = 2 * ROUNDS
    save_shape = pltpu.make_async_copy(S, shape_out, sem.at[L_S])
    shape_down = remote(S.at[:, pl.ds(0, TY)], gdS, S_GD, R_GD, (px_prev, py))
    shape_right = remote(c0S, grS, S_GR, R_GR, (px, py_prev))

    def spans(i):
        return pl.ds(pl.multiple_of(i * TY, TY), TY)

    def lanes(c):
        return slice(c * V, (c + 1) * V)

    def scatter(c):
        SF[TY : NODES - TY, lanes(c)] = dot(ONE[TY : NODES - TY], F2[:, lanes(c)])

    def advance(c, i, a, b):
        at = spans(i)
        r = R[c, at] - SF[at, lanes(c)]
        R[c, at] = r
        d = a * D[c, at] + (INV[at] * b) * r
        D[c, at] = d
        X[c, at] = X[c, at] + d

    def begin(c, i):
        at = spans(i)
        d = INV[at] * (1.0 / THETA) * R[c, at]
        D[c, at] = d
        X[c, at] = d

    def turn(c, i, a, b):
        at = spans(i)
        inv = INV[at]
        r = R[c, at] - SF[at, lanes(c)]
        x = X[c, at] + (a * D[c, at] + (inv * b) * r)
        S[c, at] = x
        r = x - T[c, at]
        R[c, at] = r
        d = inv * r * (1.0 / THETA)
        D[c, at] = d
        X[c, at] = d

    def each(fn, lo, hi):
        def body(i, carry):
            fn(i)
            return carry

        lax.fori_loop(lo, hi, body, 0)

    def stencil(c, i, par, above, below):
        at = spans(i)
        row = iota((TY, V), 0)
        d = D[c, at]
        left = jnp.where(row == 0, lf[par, c, pl.ds(i, 1), :], pltpu.roll(d, 1, 0))
        right = jnp.where(row == TY - 1, rt[par, c, pl.ds(i, 1), :], pltpu.roll(d, TY - 1, 0))
        near = WD[at] * above + WD[spans(i + 1)] * below + WL[at] * left + WR[at] * right
        R[c, at] = R[c, at] - (GD[at] * d - near)

    def rims(c, par):
        which = par * 3 + c
        return (
            remote(
                D.at[c, pl.ds((TX - 1) * TY, TY)], up.at[par, c], S_UP + c, R_UP + which, (px_next, py)
            ),
            remote(D.at[c, pl.ds(0, TY)], dn.at[par, c], S_DN + c, R_DN + which, (px_prev, py)),
        )

    def early(c):
        return (2, 1, 1)[c]

    def sides(c, par):
        which = par * 3 + c
        return (
            remote(cr.at[c], lf.at[par, c], S_LF + c, R_LF + which, (px, py_next)),
            remote(cl.at[c], rt.at[par, c], S_RT + c, R_RT + which, (px, py_prev)),
        )

    for c in range(3):
        begin(c, 0)
        begin(c, TX - 1)
        for copy in rims(c, 0)[: early(c)]:
            copy.start()
    inner = slice(TY, NODES - TY)
    INV[inner] = 1.0 / (GD[inner] + dot(ONE[inner], slot_sum))

    def stretches(view, store):
        at_a_, at_b_ = ends(cab_s[...], h0)
        inc_ = (at_a_ - at_b_).astype(BF16)
        total = None
        for c in range(3):
            out = None
            for part in split3(view[c].reshape(128, V)):
                piece = lax.dot_general(
                    inc_, part, (((0,), (0,)), ((), ())), preferred_element_type=F32
                )
                out = piece if out is None else out + piece
            if store:
                stS[c] = out
            else:
                term = out * stS[c]
                total = term if total is None else total + term
        return total

    def round_(t, carry):
        par = t % 2
        first, middle = t == 0, t == ROUNDS
        usual = jnp.logical_and(t != 0, t != ROUNDS)
        final, half_way = t == last - 1, t == ROUNDS - 1
        a_prev, b_prev = coef_of((t + ROUNDS - 1) % ROUNDS)
        a_next, b_next = coef_of(t % ROUNDS)

        for c in range(3):
            @pl.when(first)
            def _():
                each(lambda i: begin(c, i), 1, TX - 1)

            @pl.when(usual)
            def _():
                scatter(c)
                each(lambda i: advance(c, i, a_prev, b_prev), 1, TX - 1)

            @pl.when(middle)
            def _():
                scatter(c)
                each(lambda i: turn(c, i, a_prev, b_prev), 1, TX - 1)

            for i in range(TX):
                cl[c, i : i + 1] = D[c, i * TY : i * TY + 1]
                cr[c, i : i + 1] = D[c, (i + 1) * TY - 1 : (i + 1) * TY]
            for copy in sides(c, par):
                copy.start()

        for c in range(3):
            wait_bytes(recv1.at[c, pl.ds(0, half - 1)], R_P1 + c)
            high, low = split2(recv1[c].reshape(SLOTS, V))
            matrix = L3[...]
            put(Fs, c, dot(matrix, jnp.concatenate([high, high], 0)) + dot(matrix[:, :SLOTS], low))
            for h, q in peers:
                to = h * half + q
                remote(
                    Fs.at[c, to], frecv.at[par, c, py], S_P2 + c, R_P2 + par * 3 + c, (px, to)
                ).start()
            frecv[par, c, py] = Fs[c, py]
            for copy in rims(c, par)[early(c) :]:
                copy.start()

        @pl.when(first)
        def _():
            wait_bytes(dq_s.at[pl.ds(0, n_py - 1)], S_DQ)
            load_t.wait()
            gather(T, t_l)

        @pl.when(middle)
        def _():
            for c in range(3):
                for i in range(TX):
                    c0S[c, i : i + 1] = S[c, i * TY : i * TY + 1]
            save_shape.start()
            send_all(XS, recvS, S_SH, R_SH)

        @pl.when(t == ROUNDS + 1)
        def _():
            shape_down.start()
            shape_right.start()

        @pl.when(t == ROUNDS + 3)
        def _():
            wait_bytes(recvS.at[:, pl.ds(0, n_py - 1)], R_SH)
            wait_bytes(recvS.at[:, pl.ds(0, n_py - 1)], S_SH)
            stretches(recvS, True)

        for c in range(3):
            for copy in sides(c, par):
                copy.wait()
            each(
                lambda i: stencil(c, i, par, D[c, spans(i - 1)], D[c, spans(i + 1)]), 1, TX - 1
            )

        for c in range(3):
            for copy in rims(c, par):
                copy.wait()
            stencil(c, 0, par, up[par, c], D[c, spans(1)])
            stencil(c, TX - 1, par, D[c, spans(TX - 2)], dn[par, c])
            gather(R, rg_l, (c,))
            wait_bytes(recv1.at[c, pl.ds(0, half - 1)], S_P1 + c)
            wait_bytes(frecv.at[0, c, pl.ds(0, n_py - 1)], R_P2 + par * 3 + c)
            high, low = split2((frecv[par, c, 0:half] + frecv[par, c, half:]).reshape(SLOTS, V))
            F2[0:SLOTS, lanes(c)] = high
            F2[SLOTS:, lanes(c)] = low
            at_node = dot(CR[...], F2[:, lanes(c)])
            r = rg_l[c] - at_node[:SLOTS]
            d = a_next * d_l[c] + (b_next * inv_l[...]) * r
            x_l[c] = x_l[c] + d
            d_l[c] = d

            @pl.when(half_way)
            def _():
                put(XS, c, x_l[c])
                d_l[c] = inv_l[...] * (x_l[c] - t_l[c]) * (1.0 / THETA)
                x_l[c] = d_l[c]

            @pl.when(jnp.logical_not(final))
            def _():
                put(Y, c, d_l[c])
                send_lent(c)

            SF[0:TY, lanes(c)] = at_node[SLOTS : SLOTS + TY]
            SF[NODES - TY :, lanes(c)] = at_node[SLOTS + TY :]

            @pl.when(half_way)
            def _():
                turn(c, 0, a_next, b_next)
                turn(c, TX - 1, a_next, b_next)

            @pl.when(jnp.logical_not(half_way))
            def _():
                advance(c, 0, a_next, b_next)
                advance(c, TX - 1, a_next, b_next)

            @pl.when(jnp.logical_not(final))
            def _():
                for copy in rims(c, 1 - par)[: early(c)]:
                    copy.start()

            @pl.when(final)
            def _():
                put(Y, c, x_l[c])
                send_comp(Y, recvA, c, S_AD, R_AD)
                remote(X.at[c, pl.ds(0, TY)], gdA.at[c], S_HD, R_HD, (px_prev, py)).start()

        for c in range(3):
            wait_bytes(frecv.at[0, c, pl.ds(0, n_py - 1)], S_P2 + c)
        return carry

    lax.fori_loop(0, last, round_, 0)

    adjoint_down = remote(X.at[:, pl.ds(0, TY)], gdA, S_HD, R_HD, (px_prev, py))
    a, b = COEF[-1]
    for c in range(3):
        scatter(c)
        each(lambda i: advance(c, i, a, b), 1, TX - 1)
    save_adjoint = pltpu.make_async_copy(X, adjoint_out, sem.at[L_A])
    save_adjoint.start()
    for c in range(3):
        for i in range(TX):
            c0A[c, i : i + 1] = X[c, i * TY : i * TY + 1]
    adjoint_right = remote(c0A, grA, S_HR, R_HR, (px, py_prev))
    adjoint_right.start()


    def lane_sums(values):
        ones = jnp.ones((8, V), BF16)
        out = None
        for part in split3(values):
            piece = dot_t(ones, part)
            out = piece if out is None else out + piece
        return out[0:1] * (-1.0 / V)

    shape_down.wait()
    shape_right.wait()

    def down(i, below_s, below_a):
        at = spans(i)
        total = None
        for c in range(3):
            term = (X[c, at] - below_a(c)) * (S[c, at] - below_s(c))
            total = term if total is None else total + term
        PD[at] = total

    each(
        lambda i: down(i, lambda c: S[c, spans(i + 1)], lambda c: X[c, spans(i + 1)]), 0, TX - 1
    )
    adjoint_right.wait()

    def beside(i):
        at = spans(i)
        row = iota((TY, V), 0)
        total = None
        for c in range(3):
            s, x = S[c, at], X[c, at]
            s_next = jnp.where(row == TY - 1, grS[c, pl.ds(i, 1), :], pltpu.roll(s, TY - 1, 0))
            x_next = jnp.where(row == TY - 1, grA[c, pl.ds(i, 1), :], pltpu.roll(x, TY - 1, 0))
            term = (x - x_next) * (s - s_next)
            total = term if total is None else total + term
        PR[at] = total

    each(beside, 0, TX)
    right_sums = lane_sums(PR[...])
    adjoint_down.wait()
    down(TX - 1, lambda c: gdS[c], lambda c: gdA[c])
    down_sums = lane_sums(PD[...])
    for i in range(TX):
        lanes = slice(i * TY, (i + 1) * TY)
        down_out[i : i + 1] = down_sums[:, lanes]
        right_out[i : i + 1] = right_sums[:, lanes]
    down_out[...] = jnp.where(gi < n_px * TX - 1, down_out[...], 0.0)
    right_out[...] = jnp.where(gj < n_py * TY - 1, right_out[...], 0.0)

    wait_bytes(recvA.at[:, pl.ds(0, n_py - 1)], R_AD)
    long_sums = lane_sums(stretches(recvA, False))
    long_out[...] = jnp.where(live, long_sums, 0.0)
    wait_bytes(recvA.at[:, pl.ds(0, n_py - 1)], S_AD)
    save_shape.wait()
    save_adjoint.wait()


def save_kernel(shape_in, adjoint_in, down_in, right_in, long_in, *refs):
    outs, (shape_v, adjoint_v, down_v, right_v, long_v, sem) = refs[:5], refs[5:]
    parts = 4
    rows = NODES // parts
    moves = []
    for src, held, dst in ((shape_in, shape_v, outs[0]), (adjoint_in, adjoint_v, outs[1])):
        for p in range(parts):
            at = (slice(None), pl.ds(p * rows, rows))
            moves.append((src.at[at], held.at[at], dst.at[at]))
    moves += [(down_in, down_v, outs[2]), (right_in, right_v, outs[3]), (long_in, long_v, outs[4])]
    fetch = [pltpu.make_async_copy(a, b, sem.at[0, k]) for k, (a, b, _) in enumerate(moves)]
    store = [pltpu.make_async_copy(b, c, sem.at[1, k]) for k, (_, b, c) in enumerate(moves)]
    for copy in fetch:
        copy.start()
    for k, copy in enumerate(fetch):
        copy.wait()
        store[k].start()
    for copy in store:
        copy.wait()


def per_device(
    n_px, n_py,
    loads, targets, anchor, q_down, q_right, send_rows, cable_a, cable_b, cable_count, cable_q,
):
    half = n_py // 2
    field = (3, NODES, V)
    vmem = pl.BlockSpec(memory_space=pltpu.VMEM)
    smem = pl.BlockSpec(memory_space=pltpu.SMEM)
    anywhere = pl.BlockSpec(memory_space=pl.ANY)

    def scratch(*shape, dtype=F32):
        return pltpu.VMEM(shape, dtype)

    lent = (3, half, 8, V)
    results = pl.pallas_call(
        functools.partial(kernel, n_px, n_py),
        out_shape=(
            jax.ShapeDtypeStruct(field, F32),
            jax.ShapeDtypeStruct(field, F32),
            jax.ShapeDtypeStruct((TX, TY), F32),
            jax.ShapeDtypeStruct((TX, TY), F32),
            jax.ShapeDtypeStruct((1, 128), F32),
        ),
        in_specs=[anywhere] * 5 + [smem] + [anywhere] * 3 + [smem, anywhere],
        out_specs=(anywhere, anywhere, vmem, vmem, vmem),
        scratch_shapes=[
            scratch(*field),
            scratch(*field),
            scratch(*field),
            scratch(*field),
            scratch(*field),
            scratch(NODES, 3 * V),
            scratch(NODES, V),
            scratch(NODES + TY, V),
            scratch(NODES, V),
            scratch(NODES, V),
            scratch(NODES, V),
            scratch(NODES, 2 * SLOTS, dtype=BF16),
            scratch(2 * SLOTS, 3 * V, dtype=BF16),
            scratch(SLOTS + 2 * TY, 2 * SLOTS, dtype=BF16),
            scratch(128, 2 * SLOTS, dtype=BF16),
            scratch(128, 128),
            scratch(128, 128),
            scratch(3, SLOTS, V),
            scratch(3, SLOTS, V),
            scratch(3, SLOTS, V),
            scratch(3, SLOTS, V),
            scratch(SLOTS, V),
            scratch(*lent),
            scratch(*lent),
            scratch(*lent),
            scratch(3, n_py, 8, V),
            scratch(3, n_py, 8, V),
            scratch(3, n_py, 8, V),
            scratch(2, 3, n_py, 8, V),
            scratch(2, 3, TY, V),
            scratch(2, 3, TY, V),
            scratch(2, 3, TX, V),
            scratch(2, 3, TX, V),
            scratch(3, TX, V),
            scratch(3, TX, V),
            scratch(8, 128),
            scratch(8, 128),
            scratch(n_py, 8, 128),
            scratch(n_py, 8, 128),
            scratch(8, 128),
            scratch(8, 128),
            scratch(TX, 128),
            scratch(TX, 128),
            scratch(3, TY, V),
            scratch(3, TX, V),
            scratch(3, TY, V),
            scratch(3, TX, V),
            scratch(3, TX, V),
            scratch(3, TX, V),
            scratch(3, 128, V),
            scratch(NODES, V),
            scratch(NODES, V),
            scratch(TX, TY),
            scratch(TX, TY),
            scratch(TX, TY),
            scratch(1, SLOTS, dtype=jnp.int32),
            scratch(1, 128, dtype=jnp.int32),
            scratch(1, 128, dtype=jnp.int32),
            scratch(1, 128),
            pltpu.SemaphoreType.DMA((N_SEM,)),
        ],
        compiler_params=pltpu.CompilerParams(
            collective_id=0, has_side_effects=True, vmem_limit_bytes=LIMIT
        ),
        name="cable_net",
    )(
        loads.reshape(field),
        targets.reshape(field),
        anchor,
        q_down,
        q_right,
        send_rows,
        send_rows,
        cable_a,
        cable_b,
        cable_count,
        cable_q,
    )
    shape_field, adjoint_field, grad_down, grad_right, grad_long = pl.pallas_call(
        save_kernel,
        out_shape=[jax.ShapeDtypeStruct(r.shape, F32) for r in results],
        in_specs=[anywhere] * 5,
        out_specs=[anywhere] * 5,
        scratch_shapes=[pltpu.VMEM(r.shape, F32) for r in results]
        + [pltpu.SemaphoreType.DMA((2, 11))],
        compiler_params=pltpu.CompilerParams(vmem_limit_bytes=LIMIT),
        name="save",
    )(*results)
    tile = (3, TX, TY, V)
    return shape_field.reshape(tile), adjoint_field.reshape(tile), grad_down, grad_right, grad_long


def solution(mesh):
    field = P(None, "px", "py", None)
    flat = P("px", "py")
    return jax.shard_map(
        functools.partial(per_device, mesh.shape["px"], mesh.shape["py"]),
        mesh=mesh,
        in_specs=(field, field) + (flat,) * 8,
        out_specs=(field, field, flat, flat, flat),
        check_vma=False,
    )
```

```python
import functools

import jax
import jax.numpy as jnp
from jax import lax
from jax.experimental import pallas as pl
from jax.experimental.pallas import tpu as pltpu
from jax.sharding import PartitionSpec as P

MESH = pl.DeviceIdType.MESH
F32 = jnp.float32
BF16 = jnp.bfloat16
HIGHEST = lax.Precision.HIGHEST

STEPS = 7
ROUNDS = STEPS - 1
TX, TY, V = 16, 64, 128
NODES = TX * TY
SLOTS = 64
LOW, HIGH = 0.05, 2.0
LIMIT = 60 << 20
THETA = (HIGH + LOW) / 2.0
DELTA = (HIGH - LOW) / 2.0


def coefficients():
    sigma = THETA / DELTA
    rho = 1.0 / sigma
    pairs = []
    for _ in range(ROUNDS):
        rho_new = 1.0 / (2.0 * sigma - rho)
        pairs.append((rho_new * rho, 2.0 * rho_new / DELTA))
        rho = rho_new
    return pairs


COEF = coefficients()


def coef_of(round_):
    a, b = (jnp.float32(value) for value in COEF[-1])
    for k in range(ROUNDS - 1):
        a = jnp.where(round_ == k, jnp.float32(COEF[k][0]), a)
        b = jnp.where(round_ == k, jnp.float32(COEF[k][1]), b)
    return a, b


def split2(x):
    high = x.astype(BF16)
    return high, (x - high.astype(F32)).astype(BF16)


def split3(x):
    high = x.astype(BF16)
    rest = x - high.astype(F32)
    mid = rest.astype(BF16)
    return high, mid, (rest - mid.astype(F32)).astype(BF16)


def dot(a, b):
    return jnp.dot(a, b, preferred_element_type=F32)


def dot_t(a, b, precision=None):
    return lax.dot_general(
        a, b, (((1,), (1,)), ((), ())), precision=precision, preferred_element_type=F32
    )


def iota(shape, dim):
    return lax.broadcasted_iota(jnp.int32, shape, dim)


(
    S_P1, R_P1, S_P2, R_P2, S_UP, R_UP, S_DN, R_DN, S_LF, R_LF, S_RT, R_RT,
    ONES,
) = range(0, 78, 6)
(
    S_CAB, R_CAB, S_DQ, R_DQ, S_QD, R_QD, S_QR, R_QR, S_SH, R_SH, S_AD, R_AD,
    S_GD, R_GD, S_GR, R_GR, S_HD, R_HD, S_HR, R_HR, L_B, L_T, L_S, L_A,
    L_0, L_1, L_2, L_3, L_4, L_5, L_6,
) = range(ONES, ONES + 31)
N_SEM = ONES + 31


def kernel(
    n_px, n_py,
    loads, targets, anchor_h, q_down_h, q_right_h, rows_s, rows_h, cab_a_h, cab_b_h, count, cab_q_h,
    shape_out, adjoint_out, down_out, right_out, long_out,
    R, D, X, S, T, SF, GD, WD, WR, WL, INV, ONE, F2, CR, L3, IO, IP,
    rg_l, d_l, x_l, t_l, inv_l, Y, XS, recv1, recvS, recvA, Fs, frecv,
    ud, lf, rt, cl, cr, cab_s, cab_r, dq_s, dq_r, qd_s, qd_r, qr_s, qr_r,
    gdS, grS, gdA, grA, c0S, c0A, stS, PD, PR,
    anchor, q_down, q_right, rows_v, cab_a, cab_b, cab_q, sem,
):
    px = lax.axis_index("px")
    py = lax.axis_index("py")
    half = n_py // 2
    h0 = py // half
    q0 = py % half
    px_next, px_prev = (px + 1) % n_px, (px + n_px - 1) % n_px
    py_next, py_prev = (py + 1) % n_py, (py + n_py - 1) % n_py

    def remote(src, dst, s, r, to):
        return pltpu.make_async_remote_copy(
            src, dst, sem.at[s], sem.at[r], device_id=to, device_id_type=MESH
        )

    def wait_bytes(view, s):
        pltpu.make_async_copy(view, view, sem.at[s]).wait()

    load_b = pltpu.make_async_copy(loads, R, sem.at[L_B])
    load_t = pltpu.make_async_copy(targets, T, sem.at[L_T])
    small = [
        pltpu.make_async_copy(src, dst, sem.at[s])
        for src, dst, s in (
            (cab_a_h, cab_a, L_0), (cab_b_h, cab_b, L_1),
            (cab_q_h, cab_q, L_3), (q_down_h, q_down, L_4), (q_right_h, q_right, L_5),
            (rows_h, rows_v, L_2), (anchor_h, anchor, L_6),
        )
    ]
    for copy in small:
        copy.start()
    load_b.start()
    load_t.start()

    barrier = pltpu.get_barrier_semaphore()
    for i in range(1, n_py):
        pl.semaphore_signal(barrier, inc=1, device_id=(px, (py + i) % n_py), device_id_type=MESH)
    pl.semaphore_signal(barrier, inc=1, device_id=(px_next, py), device_id_type=MESH)
    pl.semaphore_signal(barrier, inc=1, device_id=(px_prev, py), device_id_type=MESH)

    wide = half // 2
    y0, c0 = q0 // 2, q0 % 2
    order = sorted(
        (v for v in ((dx, dy, dc) for dx in (0, 1) for dy in range(wide) for dc in (0, 1)) if any(v)),
        key=lambda v: -(2 * v[0] + min(v[1], wide - v[1])),
    )

    def other(dx, dy, dc):
        return (h0 + dx) % 2, (y0 + dy) % wide * 2 + (c0 + dc) % 2

    peers = [other(*v) for v in order]
    near_peers = [other(*v) for v in order if v[0] == 0]

    for copy in small:
        copy.wait()

    live = iota((1, 128), 1) < count[0, 0]
    q_live = jnp.where(live, cab_q[...], 0.0)
    row8 = iota((8, 128), 0)
    cab_s[...] = jnp.where(
        row8 == 0,
        cab_a[...].astype(F32),
        jnp.where(row8 == 1, cab_b[...].astype(F32), jnp.where(row8 == 2, q_live, 0.0)),
    )
    m_id = iota((128, 128), 0)
    code = (m_id // 8 * 4 + m_id % 4).astype(F32)
    m_half = m_id % 8 // 4

    def ends(values, which):
        mine = m_half == which
        at_a = jnp.where(mine & (code == values[0:1]), 1.0, 0.0)
        at_b = jnp.where(mine & (code == values[1:2]), 1.0, 0.0)
        return at_a, at_b

    at_a, at_b = ends(cab_s[...], h0)
    slot_q = jnp.sum((at_a + at_b) * q_live, axis=1, keepdims=True)
    dq_s[...] = jnp.broadcast_to(slot_q, (128, 128)).reshape(n_py, 8, 128)
    qd_s[...] = jnp.concatenate(
        [jnp.broadcast_to(q_down[TX - 1 : TX, :], (8, TY)), jnp.zeros((8, 128 - TY), F32)], axis=1
    )
    qr_s[...] = jnp.concatenate([q_right[...], jnp.zeros((TX, 128 - TY), F32)], axis=1)

    p_id, l_id = iota((SLOTS, 2 * SLOTS), 0), iota((SLOTS, 2 * SLOTS), 1) % SLOTS
    perm = jnp.where(p_id == (l_id // 8 + half * (l_id % 8 // 4)) * 4 + l_id % 4, 1.0, 0.0)
    row_f = jnp.broadcast_to(rows_v[...].astype(F32), (8, SLOTS))
    in_lanes = jnp.dot(row_f, perm, precision=HIGHEST, preferred_element_type=F32)[0:1]
    in_rows = lax.dot_general(
        perm[:, :SLOTS], row_f, (((0,), (1,)), ((), ())), precision=HIGHEST, preferred_element_type=F32
    )[:, 0:1]
    CR[0:SLOTS] = jnp.where(
        jnp.broadcast_to(in_rows, (SLOTS, 2 * SLOTS)) == in_lanes, 1.0, 0.0
    ).astype(BF16)

    def one_hot(i, carry):
        node = (iota((TY, 2 * SLOTS), 0) + i * TY).astype(F32)
        ONE[pl.ds(pl.multiple_of(i * TY, TY), TY)] = jnp.where(node == in_lanes, 1.0, 0.0).astype(BF16)
        return carry

    lax.fori_loop(0, TX, one_hot, 0)
    CR[SLOTS : SLOTS + TY] = ONE[0:TY]
    CR[SLOTS + TY :] = ONE[NODES - TY :]

    pl.semaphore_wait(barrier, n_py + 1)

    for h, q in peers:
        t = h * half + q
        remote(dq_s.at[t], dq_r.at[py], S_DQ, R_DQ, (px, t)).start()
    cab_copy = remote(cab_s, cab_r, S_CAB, R_CAB, (px, (py + half) % n_py))
    qd_copy = remote(qd_s, qd_r, S_QD, R_QD, (px_next, py))
    qr_copy = remote(qr_s, qr_r, S_QR, R_QR, (px, py_next))
    cab_copy.start()
    qd_copy.start()
    qr_copy.start()
    dq_r[py] = dq_s[py]

    qd_copy.wait()
    qr_copy.wait()
    gi = iota((TX, TY), 0) + px * TX
    gj = iota((TX, TY), 1) + py * TY
    w_down = jnp.where(gi < n_px * TX - 1, q_down[...], 0.0)
    w_right = jnp.where(gj < n_py * TY - 1, q_right[...], 0.0)
    prev_down = jnp.where(px > 0, qd_r[0:1, :TY], 0.0)
    prev_right = jnp.where(py > 0, qr_r[:, TY - 1 : TY], 0.0)
    w_up = jnp.concatenate([prev_down, w_down[:-1]], 0)
    w_left = jnp.concatenate([prev_right, w_right[:, :-1]], 1)
    diag = anchor[...] + w_down + w_up + w_right + w_left
    stacked = jnp.concatenate(
        [diag, w_down, w_right, w_left, jnp.broadcast_to(prev_down, (8, TY))], 0
    )
    eye = jnp.where(iota((TY, TY), 0) == iota((TY, TY), 1), 1.0, 0.0)
    columns = dot_t(eye, stacked, HIGHEST)

    def spread(col):
        return jnp.broadcast_to(columns[:, col : col + 1], (TY, V))

    WD[0:TY] = spread(4 * TX)
    for i in range(TX):
        at = pl.ds(i * TY, TY)
        GD[at] = spread(i)
        WD[pl.ds((i + 1) * TY, TY)] = spread(TX + i)
        WR[at] = spread(2 * TX + i)
        WL[at] = spread(3 * TX + i)

    cab_copy.wait()
    pa, pb = ends(cab_r[...], 1 - h0)
    inc_own, inc_other = at_a - at_b, pa - pb
    IO[...] = inc_own
    IP[...] = inc_other
    of_half = pl.ds(pl.multiple_of(h0 * SLOTS, SLOTS), SLOTS)
    matrix = dot_t(inc_own * q_live, IO[of_half], HIGHEST) + dot_t(
        inc_other * cab_r[2:3], IP[of_half], HIGHEST
    )
    L3[...] = jnp.concatenate([matrix, matrix - matrix.astype(BF16).astype(F32)], 1).astype(BF16)

    def gather(src, dst, comps=(0, 1, 2)):
        def rows_of(w, carry):
            for e in range(8):
                node = rows_s[0, (w + half * (e // 4)) * 4 + e % 4]
                for c in comps:
                    dst[c, pl.ds(w * 8 + e, 1), :] = src[c, pl.ds(node, 1), :]
            return carry

        lax.fori_loop(0, half, rows_of, 0)

    def gather_diag(w, carry):
        for e in range(8):
            node = rows_s[0, (w + half * (e // 4)) * 4 + e % 4]
            inv_l[pl.ds(w * 8 + e, 1), :] = GD[pl.ds(node, 1), :]
        return carry

    def send_all(src, dst, s, r):
        for h, q in peers:
            remote(src.at[:, q], dst.at[:, py], s, r, (px, h * half + q)).start()
        for c in range(3):
            dst[c, py] = src[c, q0]

    def send_comp(src, dst, c, s, r):
        for h, q in peers:
            remote(src.at[c, q], dst.at[c, py], s, r, (px, h * half + q)).start()
        dst[c, py] = src[c, q0]

    def send_lent(c):
        for h, q in near_peers:
            remote(Y.at[c, q], recv1.at[c, q0], S_P1 + c, R_P1 + c, (px, h * half + q)).start()
        recv1[c, q0] = Y[c, q0]

    def put(dst, c, value):
        dst[c] = value.reshape(dst.shape[1], 8, V)

    lax.fori_loop(0, half, gather_diag, 0)
    load_b.wait()
    gather(R, rg_l)

    wait_bytes(dq_r.at[pl.ds(0, n_py - 1)], R_DQ)
    slot_sum = (dq_r[0:half] + dq_r[half:]).reshape(SLOTS, V)
    slot_sum = jnp.concatenate(split2(slot_sum), 0)
    inv_l[...] = 1.0 / (inv_l[...] + dot(CR[0:SLOTS], slot_sum))
    for c in range(3):
        first = inv_l[...] * rg_l[c] * (1.0 / THETA)
        d_l[c] = first
        x_l[c] = first
        put(Y, c, first)
        send_lent(c)
    on_rims = dot(CR[SLOTS:], slot_sum)
    INV[0:TY] = 1.0 / (GD[0:TY] + on_rims[:TY])
    INV[NODES - TY :] = 1.0 / (GD[NODES - TY :] + on_rims[TY:])

    last = 2 * ROUNDS
    save_shape = pltpu.make_async_copy(S, shape_out, sem.at[L_S])
    shape_down = remote(S.at[:, pl.ds(0, TY)], gdS, S_GD, R_GD, (px_prev, py))
    shape_right = remote(c0S, grS, S_GR, R_GR, (px, py_prev))

    def spans(i):
        return pl.ds(pl.multiple_of(i * TY, TY), TY)

    def lanes(c):
        return slice(c * V, (c + 1) * V)

    def scatter(c):
        SF[TY : NODES - TY, lanes(c)] = dot(ONE[TY : NODES - TY], F2[:, lanes(c)])

    def advance(c, i, a, b):
        at = spans(i)
        r = R[c, at] - SF[at, lanes(c)]
        R[c, at] = r
        d = a * D[c, at] + (INV[at] * b) * r
        D[c, at] = d
        X[c, at] = X[c, at] + d

    def begin(c, i):
        at = spans(i)
        d = INV[at] * (1.0 / THETA) * R[c, at]
        D[c, at] = d
        X[c, at] = d

    def turn(c, i, a, b):
        at = spans(i)
        inv = INV[at]
        r = R[c, at] - SF[at, lanes(c)]
        x = X[c, at] + (a * D[c, at] + (inv * b) * r)
        S[c, at] = x
        r = x - T[c, at]
        R[c, at] = r
        d = inv * r * (1.0 / THETA)
        D[c, at] = d
        X[c, at] = d

    def each(fn, lo, hi):
        def body(i, carry):
            fn(i)
            return carry

        lax.fori_loop(lo, hi, body, 0)

    def stencil(c, i, par, above, below):
        at = spans(i)
        row = iota((TY, V), 0)
        d = D[c, at]
        left = jnp.where(row == 0, lf[par, c, pl.ds(i, 1), :], pltpu.roll(d, 1, 0))
        right = jnp.where(row == TY - 1, rt[par, c, pl.ds(i, 1), :], pltpu.roll(d, TY - 1, 0))
        near = WD[at] * above + WD[spans(i + 1)] * below + WL[at] * left + WR[at] * right
        R[c, at] = R[c, at] - (GD[at] * d - near)

    def rims(c, par):
        def one(s, is_next):
            row = pl.multiple_of(is_next * ((TX - 1) * TY), TY)
            to = (px + n_px - 1 + 2 * is_next) % n_px
            r = R_UP + (1 - is_next) * (R_DN - R_UP) + par * 3 + c
            return remote(
                D.at[c, pl.ds(row, TY)], ud.at[par, c, 1 - is_next], s + c, r, (to, py)
            )

        odd = px % 2
        return one(S_UP, odd), one(S_DN, 1 - odd)

    def early(c):
        return (2, 1, 1)[c]

    def sides(c, par):
        which = par * 3 + c
        return (
            remote(cr.at[c], lf.at[par, c], S_LF + c, R_LF + which, (px, py_next)),
            remote(cl.at[c], rt.at[par, c], S_RT + c, R_RT + which, (px, py_prev)),
        )

    for c in range(3):
        begin(c, 0)
        begin(c, TX - 1)
        for copy in rims(c, 0)[: early(c)]:
            copy.start()
    inner = slice(TY, NODES - TY)
    INV[inner] = 1.0 / (GD[inner] + dot(ONE[inner], slot_sum))

    def stretches(view, store):
        at_a_, at_b_ = ends(cab_s[...], h0)
        inc_ = (at_a_ - at_b_).astype(BF16)
        total = None
        for c in range(3):
            out = None
            for part in split3(view[c].reshape(128, V)):
                piece = lax.dot_general(
                    inc_, part, (((0,), (0,)), ((), ())), preferred_element_type=F32
                )
                out = piece if out is None else out + piece
            if store:
                stS[c] = out
            else:
                term = out * stS[c]
                total = term if total is None else total + term
        return total

    def round_(t, carry):
        par = t % 2
        first, middle = t == 0, t == ROUNDS
        usual = jnp.logical_and(t != 0, t != ROUNDS)
        final, half_way = t == last - 1, t == ROUNDS - 1
        a_prev, b_prev = coef_of((t + ROUNDS - 1) % ROUNDS)
        a_next, b_next = coef_of(t % ROUNDS)

        for c in range(3):
            @pl.when(first)
            def _():
                each(lambda i: begin(c, i), 1, TX - 1)

            @pl.when(usual)
            def _():
                scatter(c)
                each(lambda i: advance(c, i, a_prev, b_prev), 1, TX - 1)

            @pl.when(middle)
            def _():
                scatter(c)
                each(lambda i: turn(c, i, a_prev, b_prev), 1, TX - 1)

            for i in range(TX):
                cl[c, i : i + 1] = D[c, i * TY : i * TY + 1]
                cr[c, i : i + 1] = D[c, (i + 1) * TY - 1 : (i + 1) * TY]
            for copy in sides(c, par):
                copy.start()

        for c in range(3):
            wait_bytes(recv1.at[c, pl.ds(0, half - 1)], R_P1 + c)
            high, low = split2(recv1[c].reshape(SLOTS, V))
            matrix = L3[...]
            put(Fs, c, dot(matrix, jnp.concatenate([high, high], 0)) + dot(matrix[:, :SLOTS], low))
            for h, q in peers:
                to = h * half + q
                remote(
                    Fs.at[c, to], frecv.at[par, c, py], S_P2 + c, R_P2 + par * 3 + c, (px, to)
                ).start()
            frecv[par, c, py] = Fs[c, py]
            for copy in rims(c, par)[early(c) :]:
                copy.start()

        @pl.when(first)
        def _():
            wait_bytes(dq_s.at[pl.ds(0, n_py - 1)], S_DQ)
            load_t.wait()
            gather(T, t_l)

        @pl.when(middle)
        def _():
            for c in range(3):
                for i in range(TX):
                    c0S[c, i : i + 1] = S[c, i * TY : i * TY + 1]
            save_shape.start()
            send_all(XS, recvS, S_SH, R_SH)

        @pl.when(t == ROUNDS + 1)
        def _():
            shape_down.start()
            shape_right.start()

        @pl.when(t == ROUNDS + 3)
        def _():
            wait_bytes(recvS.at[:, pl.ds(0, n_py - 1)], R_SH)
            wait_bytes(recvS.at[:, pl.ds(0, n_py - 1)], S_SH)
            stretches(recvS, True)

        for c in range(3):
            for copy in sides(c, par):
                copy.wait()
            each(
                lambda i: stencil(c, i, par, D[c, spans(i - 1)], D[c, spans(i + 1)]), 1, TX - 1
            )

        for c in range(3):
            for copy in rims(c, par):
                copy.wait()
            stencil(c, 0, par, ud[par, c, 0], D[c, spans(1)])
            stencil(c, TX - 1, par, D[c, spans(TX - 2)], ud[par, c, 1])
            gather(R, rg_l, (c,))
            wait_bytes(recv1.at[c, pl.ds(0, half - 1)], S_P1 + c)
            wait_bytes(frecv.at[0, c, pl.ds(0, n_py - 1)], R_P2 + par * 3 + c)
            high, low = split2((frecv[par, c, 0:half] + frecv[par, c, half:]).reshape(SLOTS, V))
            F2[0:SLOTS, lanes(c)] = high
            F2[SLOTS:, lanes(c)] = low
            at_node = dot(CR[...], F2[:, lanes(c)])
            r = rg_l[c] - at_node[:SLOTS]
            d = a_next * d_l[c] + (b_next * inv_l[...]) * r
            x_l[c] = x_l[c] + d
            d_l[c] = d

            @pl.when(half_way)
            def _():
                put(XS, c, x_l[c])
                d_l[c] = inv_l[...] * (x_l[c] - t_l[c]) * (1.0 / THETA)
                x_l[c] = d_l[c]

            @pl.when(jnp.logical_not(final))
            def _():
                put(Y, c, d_l[c])
                send_lent(c)

            SF[0:TY, lanes(c)] = at_node[SLOTS : SLOTS + TY]
            SF[NODES - TY :, lanes(c)] = at_node[SLOTS + TY :]

            @pl.when(half_way)
            def _():
                turn(c, 0, a_next, b_next)
                turn(c, TX - 1, a_next, b_next)

            @pl.when(jnp.logical_not(half_way))
            def _():
                advance(c, 0, a_next, b_next)
                advance(c, TX - 1, a_next, b_next)

            @pl.when(jnp.logical_not(final))
            def _():
                for copy in rims(c, 1 - par)[: early(c)]:
                    copy.start()

            @pl.when(final)
            def _():
                put(Y, c, x_l[c])
                send_comp(Y, recvA, c, S_AD, R_AD)
                remote(X.at[c, pl.ds(0, TY)], gdA.at[c], S_HD, R_HD, (px_prev, py)).start()

        for c in range(3):
            wait_bytes(frecv.at[0, c, pl.ds(0, n_py - 1)], S_P2 + c)
        return carry

    lax.fori_loop(0, last, round_, 0)

    adjoint_down = remote(X.at[:, pl.ds(0, TY)], gdA, S_HD, R_HD, (px_prev, py))
    a, b = COEF[-1]
    for c in range(3):
        scatter(c)
        each(lambda i: advance(c, i, a, b), 1, TX - 1)
    save_adjoint = pltpu.make_async_copy(X, adjoint_out, sem.at[L_A])
    save_adjoint.start()
    for c in range(3):
        for i in range(TX):
            c0A[c, i : i + 1] = X[c, i * TY : i * TY + 1]
    adjoint_right = remote(c0A, grA, S_HR, R_HR, (px, py_prev))
    adjoint_right.start()


    def lane_sums(values):
        ones = jnp.ones((8, V), BF16)
        out = None
        for part in split3(values):
            piece = dot_t(ones, part)
            out = piece if out is None else out + piece
        return out[0:1] * (-1.0 / V)

    shape_down.wait()
    shape_right.wait()

    def down(i, below_s, below_a):
        at = spans(i)
        total = None
        for c in range(3):
            term = (X[c, at] - below_a(c)) * (S[c, at] - below_s(c))
            total = term if total is None else total + term
        PD[at] = total

    each(
        lambda i: down(i, lambda c: S[c, spans(i + 1)], lambda c: X[c, spans(i + 1)]), 0, TX - 1
    )
    adjoint_right.wait()

    def beside(i):
        at = spans(i)
        row = iota((TY, V), 0)
        total = None
        for c in range(3):
            s, x = S[c, at], X[c, at]
            s_next = jnp.where(row == TY - 1, grS[c, pl.ds(i, 1), :], pltpu.roll(s, TY - 1, 0))
            x_next = jnp.where(row == TY - 1, grA[c, pl.ds(i, 1), :], pltpu.roll(x, TY - 1, 0))
            term = (x - x_next) * (s - s_next)
            total = term if total is None else total + term
        PR[at] = total

    each(beside, 0, TX)
    right_sums = lane_sums(PR[...])
    adjoint_down.wait()
    down(TX - 1, lambda c: gdS[c], lambda c: gdA[c])
    down_sums = lane_sums(PD[...])
    for i in range(TX):
        lanes = slice(i * TY, (i + 1) * TY)
        down_out[i : i + 1] = down_sums[:, lanes]
        right_out[i : i + 1] = right_sums[:, lanes]
    down_out[...] = jnp.where(gi < n_px * TX - 1, down_out[...], 0.0)
    right_out[...] = jnp.where(gj < n_py * TY - 1, right_out[...], 0.0)

    wait_bytes(recvA.at[:, pl.ds(0, n_py - 1)], R_AD)
    long_sums = lane_sums(stretches(recvA, False))
    long_out[...] = jnp.where(live, long_sums, 0.0)
    wait_bytes(recvA.at[:, pl.ds(0, n_py - 1)], S_AD)
    save_shape.wait()
    save_adjoint.wait()


def save_kernel(shape_in, adjoint_in, down_in, right_in, long_in, *refs):
    outs, (shape_v, adjoint_v, down_v, right_v, long_v, sem) = refs[:5], refs[5:]
    parts = 4
    rows = NODES // parts
    moves = []
    for src, held, dst in ((shape_in, shape_v, outs[0]), (adjoint_in, adjoint_v, outs[1])):
        for p in range(parts):
            at = (slice(None), pl.ds(p * rows, rows))
            moves.append((src.at[at], held.at[at], dst.at[at]))
    moves += [(down_in, down_v, outs[2]), (right_in, right_v, outs[3]), (long_in, long_v, outs[4])]
    fetch = [pltpu.make_async_copy(a, b, sem.at[0, k]) for k, (a, b, _) in enumerate(moves)]
    store = [pltpu.make_async_copy(b, c, sem.at[1, k]) for k, (_, b, c) in enumerate(moves)]
    for copy in fetch:
        copy.start()
    for k, copy in enumerate(fetch):
        copy.wait()
        store[k].start()
    for copy in store:
        copy.wait()


def per_device(
    n_px, n_py,
    loads, targets, anchor, q_down, q_right, send_rows, cable_a, cable_b, cable_count, cable_q,
):
    half = n_py // 2
    field = (3, NODES, V)
    vmem = pl.BlockSpec(memory_space=pltpu.VMEM)
    smem = pl.BlockSpec(memory_space=pltpu.SMEM)
    anywhere = pl.BlockSpec(memory_space=pl.ANY)

    def scratch(*shape, dtype=F32):
        return pltpu.VMEM(shape, dtype)

    lent = (3, half, 8, V)
    results = pl.pallas_call(
        functools.partial(kernel, n_px, n_py),
        out_shape=(
            jax.ShapeDtypeStruct(field, F32),
            jax.ShapeDtypeStruct(field, F32),
            jax.ShapeDtypeStruct((TX, TY), F32),
            jax.ShapeDtypeStruct((TX, TY), F32),
            jax.ShapeDtypeStruct((1, 128), F32),
        ),
        in_specs=[anywhere] * 5 + [smem] + [anywhere] * 3 + [smem, anywhere],
        out_specs=(anywhere, anywhere, vmem, vmem, vmem),
        scratch_shapes=[
            scratch(*field),
            scratch(*field),
            scratch(*field),
            scratch(*field),
            scratch(*field),
            scratch(NODES, 3 * V),
            scratch(NODES, V),
            scratch(NODES + TY, V),
            scratch(NODES, V),
            scratch(NODES, V),
            scratch(NODES, V),
            scratch(NODES, 2 * SLOTS, dtype=BF16),
            scratch(2 * SLOTS, 3 * V, dtype=BF16),
            scratch(SLOTS + 2 * TY, 2 * SLOTS, dtype=BF16),
            scratch(128, 2 * SLOTS, dtype=BF16),
            scratch(128, 128),
            scratch(128, 128),
            scratch(3, SLOTS, V),
            scratch(3, SLOTS, V),
            scratch(3, SLOTS, V),
            scratch(3, SLOTS, V),
            scratch(SLOTS, V),
            scratch(*lent),
            scratch(*lent),
            scratch(*lent),
            scratch(3, n_py, 8, V),
            scratch(3, n_py, 8, V),
            scratch(3, n_py, 8, V),
            scratch(2, 3, n_py, 8, V),
            scratch(2, 3, 2, TY, V),
            scratch(2, 3, TX, V),
            scratch(2, 3, TX, V),
            scratch(3, TX, V),
            scratch(3, TX, V),
            scratch(8, 128),
            scratch(8, 128),
            scratch(n_py, 8, 128),
            scratch(n_py, 8, 128),
            scratch(8, 128),
            scratch(8, 128),
            scratch(TX, 128),
            scratch(TX, 128),
            scratch(3, TY, V),
            scratch(3, TX, V),
            scratch(3, TY, V),
            scratch(3, TX, V),
            scratch(3, TX, V),
            scratch(3, TX, V),
            scratch(3, 128, V),
            scratch(NODES, V),
            scratch(NODES, V),
            scratch(TX, TY),
            scratch(TX, TY),
            scratch(TX, TY),
            scratch(1, SLOTS, dtype=jnp.int32),
            scratch(1, 128, dtype=jnp.int32),
            scratch(1, 128, dtype=jnp.int32),
            scratch(1, 128),
            pltpu.SemaphoreType.DMA((N_SEM,)),
        ],
        compiler_params=pltpu.CompilerParams(
            collective_id=0, has_side_effects=True, vmem_limit_bytes=LIMIT
        ),
        name="cable_net",
    )(
        loads.reshape(field),
        targets.reshape(field),
        anchor,
        q_down,
        q_right,
        send_rows,
        send_rows,
        cable_a,
        cable_b,
        cable_count,
        cable_q,
    )
    shape_field, adjoint_field, grad_down, grad_right, grad_long = pl.pallas_call(
        save_kernel,
        out_shape=[jax.ShapeDtypeStruct(r.shape, F32) for r in results],
        in_specs=[anywhere] * 5,
        out_specs=[anywhere] * 5,
        scratch_shapes=[pltpu.VMEM(r.shape, F32) for r in results]
        + [pltpu.SemaphoreType.DMA((2, 11))],
        compiler_params=pltpu.CompilerParams(vmem_limit_bytes=LIMIT),
        name="save",
    )(*results)
    tile = (3, TX, TY, V)
    return shape_field.reshape(tile), adjoint_field.reshape(tile), grad_down, grad_right, grad_long


def solution(mesh):
    field = P(None, "px", "py", None)
    flat = P("px", "py")
    return jax.shard_map(
        functools.partial(per_device, mesh.shape["px"], mesh.shape["py"]),
        mesh=mesh,
        in_specs=(field, field) + (flat,) * 8,
        out_specs=(field, field, flat, flat, flat),
        check_vma=False,
    )
```
